32 devices in a mesh: col: 8 (over z, y), row: 4 (over x, core).
Axes of the slice: x: 2, y: 2, z: 4, core: 2. Of those that a mesh axis runs over, the one named last changes fastest.
Arguments:
- tile_left: bfloat16 [8, 8, 1024, 64], P('col', 'row'), may hold values from -0.41992188 to 0.41992188
- tile_right: bfloat16 [8, 8, 1024, 64], P('col', 'row'), may hold values from -0.1875 to 0.1875
- row_left: bfloat16 [8, 1024, 64], P('col'), may hold values from -0.41992188 to 0.41992188
- row_right: bfloat16 [8, 1024, 64], P('col'), may hold values from -0.1875 to 0.1875
- sketch: bfloat16 [1024, 64], replicated, may hold values from -6 to 6
- panel_left: bfloat16 [8, 1024, 64], P('row'), may hold values from -0.375 to 0.375
- panel_right: bfloat16 [8, 1024, 64], P('row'), may hold values from -0.1875 to 0.1875
- pivot_inverse: bfloat16 [1024, 1024], replicated, as said below
- band_inverse: bfloat16 [8, 1024, 1024], P('row'), as said below
- link_left: bfloat16 [8, 1024, 64], P('row'), may hold values from -0.75 to 0.75
- link_right: bfloat16 [8, 1024, 64], P('row'), may hold values from -0.0625 to 0.0625
- pivot_rhs: bfloat16 [1024, 4096], P(None, 'col'), may hold values from -6 to 6
- band_rhs: bfloat16 [8, 1024, 4096], P('row', None, 'col'), may hold values from -6 to 6
- carry_in: float32 [64, 4096], P(None, 'col'), may hold values from -3 to 3
Outputs:
- pivot_solution: bfloat16 [1024, 4096], P(None, 'col')
- schur_right: float32 [8, 1024, 64], P('row', 'col')
- band_solution: bfloat16 [8, 1024, 4096], P('row', None, 'col')
- link_states: float32 [8, 64, 4096], P('row', None, 'col')
The draws below stay inside these ranges and needn't reach their ends.
Inputs may be any that keep to these rules, and one draw needn't show every extreme that they name: `pivot_inverse`: each tile is lower triangular with a positive diagonal, the inverse of a Cholesky factor of a diagonal covariance tile. `band_inverse`: each tile is lower triangular with a positive diagonal, the inverse of a Cholesky factor of a diagonal covariance tile.
All inputs are finite; a program needn't handle non-finite values.
Results may differ from the reference program's by a relative error of at most 0.0056.
Values sent between devices are 32-bit elements; how exact they have to be, the bound alone decides.
No kernel may reach another device: no remote copies, remote signals or barrier semaphores. Data moves between devices by JAX's collectives and lax.ppermute only.
A program may use at most 128 MiB of HBM per device.

```python
import jax
import jax.numpy as jnp
from jax import lax

NB = 1024
R = 64
NJ = 8
NBR = 8
RHS_TOT = 4096


def triangle_tiles(key, tile_count):
    diag_key, off_key = jax.random.split(key)
    diagonal = jax.random.uniform(diag_key, (tile_count, NB), jnp.float32, 0.6, 1.5)
    off_diagonal = jnp.clip(jax.random.normal(off_key, (tile_count, NB, NB), jnp.float32), -4.0, 4.0) * (0.5 / NB ** 0.5)
    lower_part = jnp.tril(off_diagonal, -1)
    return lower_part + diagonal[:, :, None] * jnp.eye(NB, dtype=jnp.float32)


def draw_pivot_inverse(key, part):
    return triangle_tiles(jax.random.fold_in(key, 11), 1)[0].astype(jnp.bfloat16)


def draw_band_inverse(key, part):
    return triangle_tiles(jax.random.fold_in(key, 23), NBR).astype(jnp.bfloat16)


def steps_of(own_key, extent, shards, smallest, largest):
    def one(dim, blocks):
        draws = jax.random.uniform(jax.random.fold_in(jax.random.fold_in(own_key, 6), dim), (blocks,), jnp.float32, smallest / len(shards), largest / len(shards))
        return jnp.repeat(jnp.exp(draws), extent[dim] // blocks).reshape((-1,) + (1,) * (len(extent) - dim - 1))

    factor_of = one(*shards[0])
    for cut in shards[1:]:
        factor_of = factor_of * one(*cut)
    return factor_of


def normal_values(own_key, extent, deviation, most, cuts=(), kind=jnp.bfloat16):
    loudness = steps_of(own_key, extent, cuts, -0.22, 0.18) if cuts else 1.0
    values = jax.random.normal(own_key, extent, jnp.float32) * deviation * loudness
    return jnp.minimum(jnp.maximum(values, -most), most).astype(kind)


def setup_inputs(seed: int = 0) -> dict:
    keys = jax.random.split(jax.random.key(seed), 15)
    return {
        "tile_left": normal_values(keys[0], (NJ, NBR, NB, R), 0.07, 0.41992188, ((0, 8), (1, 4))),
        "tile_right": normal_values(keys[1], (NJ, NBR, NB, R), NB ** -0.5, 0.1875, ((0, 8), (1, 4))),
        "row_left": normal_values(keys[2], (NJ, NB, R), 0.07, 0.41992188, ((0, 8),)),
        "row_right": normal_values(keys[3], (NJ, NB, R), NB ** -0.5, 0.1875, ((0, 8),)),
        "sketch": normal_values(keys[4], (NB, R), 1.0, 6.0),
        "panel_left": normal_values(keys[5], (NBR, NB, R), (4 * R) ** -0.5, 0.375, ((0, 4),)),
        "panel_right": normal_values(keys[6], (NBR, NB, R), NB ** -0.5, 0.1875, ((0, 4),)),
        "pivot_inverse": draw_pivot_inverse(jax.random.fold_in(keys[14], 71), 0),
        "band_inverse": draw_band_inverse(jax.random.fold_in(keys[14], 71), 0),
        "link_left": normal_values(keys[9], (NBR, NB, R), R ** -0.5, 0.75, ((0, 4),)),
        "link_right": normal_values(keys[10], (NBR, NB, R), (8 * NB) ** -0.5, 0.0625, ((0, 4),)),
        "pivot_rhs": normal_values(keys[11], (NB, RHS_TOT), 1.0, 6.0, ((1, 8),)),
        "band_rhs": normal_values(keys[12], (NBR, NB, RHS_TOT), 1.0, 6.0, ((0, 4), (2, 8))),
        "carry_in": normal_values(keys[13], (R, RHS_TOT), 0.5, 3.0, ((1, 8),), jnp.float32),
    }


HIGHEST_PRECISION = lax.Precision.HIGHEST

def widened(array):
    return array.astype(jnp.float32)

def reference(tile_left, tile_right, row_left, row_right, sketch, panel_left, panel_right, pivot_inverse, band_inverse, link_left, link_right, pivot_rhs, band_rhs, carry_in):
    pivot_solution = jnp.dot(pivot_inverse.astype(jnp.float32), pivot_rhs.astype(jnp.float32), preferred_element_type=jnp.float32).astype(jnp.bfloat16)
    pulled = jnp.dot(widened(pivot_inverse).T, widened(pivot_solution), precision=HIGHEST_PRECISION)
    probe_core = jnp.einsum('jnr,ns->jrs', widened(row_left), widened(sketch), precision=HIGHEST_PRECISION)
    row_wide = widened(row_left)
    row_right_wide = widened(row_right)
    identity_matrix = jnp.eye(R, dtype=jnp.float32)

    def panel_row(band_index):
        left_tiles = widened(lax.dynamic_index_in_dim(tile_left, band_index, 1, keepdims=False))
        right_tiles = widened(lax.dynamic_index_in_dim(tile_right, band_index, 1, keepdims=False))
        coupling = jnp.einsum('jnr,jns->jrs', right_tiles, row_right_wide, precision=HIGHEST_PRECISION)
        sketch_core = jnp.einsum('jrs,jst->jrt', coupling, probe_core, precision=HIGHEST_PRECISION)
        sketched = jnp.einsum('jnr,jrt->nt', left_tiles, sketch_core, precision=HIGHEST_PRECISION)
        gram_matrix = jnp.dot(sketched.T, sketched, precision=HIGHEST_PRECISION)
        gram_lower = jnp.linalg.cholesky(gram_matrix)
        inverse_low = lax.linalg.triangular_solve(gram_lower, identity_matrix.astype(gram_lower.dtype), left_side=True, lower=True)
        panel_basis = jnp.dot(sketched, inverse_low.T, precision=HIGHEST_PRECISION)
        projected = jnp.einsum('jnr,ns->jrs', left_tiles, panel_basis, precision=HIGHEST_PRECISION)
        middle = jnp.einsum('jrs,jrt->jst', coupling, projected, precision=HIGHEST_PRECISION)
        schur = jnp.einsum('jns,jst->nt', row_wide, middle, precision=HIGHEST_PRECISION)
        return (panel_basis, schur)
    panel_basis, schur_right = lax.map(panel_row, jnp.arange(NBR, dtype=jnp.int32))

    def band_step(prior_state, items):
        inverse, right_side, left_link, right_link, left_panel, right_panel, basis_tile, schur_tile = items
        panel_coeffs = jnp.dot(widened(right_panel).T, pulled, precision=HIGHEST_PRECISION)
        schur_coeffs = jnp.dot(schur_tile.T, pulled, precision=HIGHEST_PRECISION)
        panel_term = jnp.dot(widened(left_panel), panel_coeffs, precision=HIGHEST_PRECISION) - jnp.dot(basis_tile, schur_coeffs, precision=HIGHEST_PRECISION)
        reduced = (widened(right_side) - panel_term).astype(jnp.bfloat16)
        local_part = jnp.dot(inverse.astype(jnp.float32), reduced.astype(jnp.float32), preferred_element_type=jnp.float32)
        feed_columns = jnp.dot(inverse.astype(jnp.float32), left_link.astype(jnp.float32), preferred_element_type=jnp.float32)
        solved = local_part - jnp.dot(feed_columns, prior_state, precision=HIGHEST_PRECISION)
        state = jnp.dot(widened(right_link).T, solved, precision=HIGHEST_PRECISION)
        return (state, (solved.astype(jnp.bfloat16), state))
    final_state, outputs = lax.scan(band_step, carry_in, (band_inverse, band_rhs, link_left, link_right, panel_left, panel_right, panel_basis, schur_right))
    band_solution, link_states = outputs
    return (pivot_solution, schur_right, band_solution, link_states)
```

```python
import functools

import jax
import jax.numpy as jnp
from jax import lax
from jax.experimental import pallas as pl
from jax.experimental.pallas import tpu as pltpu
from jax.sharding import PartitionSpec as P

F32 = jnp.float32
BF16 = jnp.bfloat16
LANES = 128
BLOCK = 256
NN = ((1,), (0,))
NT = ((1,), (1,))
TN = ((0,), (0,))


def halves(x):
    high = x.astype(BF16)
    return high, (x - high.astype(F32)).astype(BF16)


def bdot(a, b, dims=NN):
    return lax.dot_general(a, b, (dims, ((), ())), preferred_element_type=F32)


def dot2(a, b, dims=NN):
    high, low = halves(b)
    return bdot(a, high, dims) + bdot(a, low, dims)


def dot3(a, b, dims=NN):
    ah, al = halves(a)
    bh, bl = halves(b)
    return bdot(ah, bh, dims) + (bdot(ah, bl, dims) + bdot(al, bh, dims))


def vmem_call(body, outs, scratch=(), flops=10**7, name=None, limit=16):
    return pl.pallas_call(
        body,
        out_shape=[jax.ShapeDtypeStruct(s, d) for s, d in outs],
        scratch_shapes=list(scratch),
        compiler_params=pltpu.CompilerParams(vmem_limit_bytes=limit * 2**20),
        cost_estimate=pl.CostEstimate(flops=flops, bytes_accessed=10**6, transcendentals=0),
        name=name,
    )


def blocks_of(extent):
    size = min(BLOCK, extent)
    return [(start, start + size) for start in range(0, extent, size)]


def couple_body(tl, tr, rl, rr, sk, x_own, msg):
    parity = lax.rem(lax.axis_index("col"), 2)
    rank, nb = rl.shape

    def crossed(band):
        coupling = bdot(tr[band], rr[...], NT)
        high, low = halves(coupling)
        both = bdot(jnp.concatenate([high, low], 1), tl[band], TN)
        return both[:rank] + both[rank:]

    x_own[...] = crossed(parity)
    msg[:, :nb] = crossed(1 - parity)
    probe = bdot(rl[...], sk[...], NT)
    msg[:, nb:] = jnp.concatenate([probe, jnp.zeros_like(probe)], 1)


def sketch_body(pieces, x_own, sent, got, x_pair, *rest):
    outs, part = rest[:-1], rest[-1]
    col = lax.axis_index("col")
    parity = lax.rem(col, 2)
    place = col // 2
    rank, nb = x_own.shape
    own, other = x_own[...], got[:, :nb]
    probes = jnp.concatenate([sent[:, nb : nb + rank], got[:, nb : nb + rank]], 0)
    part[...] = dot3(probes, jnp.concatenate([own, other], 0), TN)
    x_pair[pl.ds(pl.multiple_of(parity * rank, rank), rank), :] = own
    x_pair[pl.ds(pl.multiple_of((1 - parity) * rank, rank), rank), :] = other
    slab = nb // pieces
    for step in range(pieces):
        start = pl.multiple_of(jnp.bitwise_xor(place, step) * slab, slab) if pieces > 1 else 0
        outs[step][...] = part[:, pl.ds(start, slab)]


def project_body(pieces, x_pair, *rest):
    slabs, (sk, crossed, gram) = rest[:pieces], rest[pieces:]
    place = lax.axis_index("col") // 2
    slab = slabs[0].shape[1]
    for step in range(pieces):
        start = pl.multiple_of(jnp.bitwise_xor(place, step) * slab, slab) if pieces > 1 else 0
        sk[:, pl.ds(start, slab)] = slabs[step][...]
    whole = sk[...]
    crossed[...] = dot3(whole, x_pair[...], NT)
    gram[...] = lax.dot_general(
        whole, whole, (NT, ((), ())), precision=lax.Precision.HIGHEST, preferred_element_type=F32
    )


def widen_body(row_left, out):
    half = out.shape[1]
    start = pl.multiple_of(lax.rem(lax.axis_index("row"), 2) * half, half)
    out[...] = row_left[:, pl.ds(start, half)].astype(F32)


def narrow_body(groups, *refs):
    blocks, out = refs[:-1], refs[-1]
    half = blocks[0].shape[-1]
    parity = lax.rem(lax.axis_index("col"), 2)
    near_start = pl.multiple_of(lax.rem(lax.axis_index("row"), 2) * half, half)
    far_start = pl.multiple_of(half - near_start, half)
    index = 0
    for start in (near_start, far_start):
        for side in (parity, 1 - parity):
            for step in range(groups):
                out[step, side, :, pl.ds(start, half)] = blocks[index][...].astype(BF16)
                index += 1


def wide_pulled_body(wide, pulled, high_out, low_out):
    pulled_high, pulled_low = halves(pulled[...])
    for first, last in blocks_of(wide.shape[0]):
        rows = wide[first:last, :]
        product = bdot(rows, pulled_high) + bdot(rows, pulled_low)
        high, low = halves(product)
        high_out[first:last, :] = high
        low_out[first:last, :] = low


def factor_body(gram, out):
    rank = gram.shape[0]
    lanes = 2 * rank
    group = 4
    tile = 8
    rows = lax.broadcasted_iota(jnp.int32, (rank, lanes), 0)
    cols = lax.broadcasted_iota(jnp.int32, (rank, lanes), 1)
    eye = jnp.where(cols == rows + rank, 1.0, 0.0).astype(F32)
    work = jnp.concatenate([gram[...], jnp.zeros((rank, rank), F32)], 1) + eye
    done = []
    scales = []
    for start in range(0, rank, group):
        top = (start // tile) * tile
        if start == top and start:
            done.append(work[:tile])
            work = work[tile:]
        ids = rows[top:]
        height = rank - top
        columns = [
            jnp.broadcast_to(work[:, start + j : start + j + 1], (height, lanes)) for j in range(group)
        ]
        for j in range(group):
            k = start + j
            at = k - top
            pivot = columns[j][at : at + 1, :]
            inverse = 1.0 / pivot
            scales.append(lax.rsqrt(pivot))
            factor = jnp.where(ids > k, columns[j] * inverse, 0.0)
            for later in range(j + 1, group):
                columns[later] = columns[later] - factor * columns[later][at : at + 1, :]
            work = work - factor * work[at : at + 1, :]
    done.append(work)
    whole = jnp.concatenate(done, 0) * jnp.concatenate(scales, 0)
    out[...] = whole[:, rank:]


def scaled_body(groups, inverse, *rest):
    blocks, out = rest[:groups], rest[groups]
    low = inverse[...]
    width = blocks[0].shape[1]
    for step in range(groups):
        out[:, step * width : (step + 1) * width] = dot3(low, blocks[step][...])
    out[:, groups * width :] = jnp.concatenate([low, jnp.zeros_like(low)], 1)


def band_body(pr, pl_t, ll, right, pulled, inverse, rhs, base, feed, offset, gain, right_rows, red):
    rank, nb = right.shape
    coeffs = dot2(pr[...], pulled[...])
    coeffs_two = jnp.concatenate(halves(coeffs), 0)
    left = pl_t[...]
    left_two = jnp.concatenate([left, left], 0)
    for first, last in blocks_of(nb):
        term = bdot(left_two[:, first:last], coeffs_two, TN)
        red[first:last, :] = (rhs[first:last, :].astype(F32) - term).astype(BF16)
    for first, last in blocks_of(nb):
        rows = inverse[first:last, :last]
        base[first:last, :] = bdot(rows, red[:last, :])
        feed_high, feed_low = halves(bdot(rows, ll[:, :last], NT))
        feed[first:last, :] = jnp.concatenate([feed_high, feed_high, feed_low], 1)
        right_rows[:, first:last] = bdot(right[:, first:], inverse[first:, first:last])
    two = jnp.concatenate(halves(right_rows[...]), 0)
    both = bdot(two, red[...])
    offset[...] = both[:rank] + both[rank:]
    both = bdot(two, ll[...], NT)
    gain[...] = both[:rank] + both[rank:]


def spread_body(inverse, right_rows, own, other, spread, spread_gain):
    parity = lax.rem(lax.axis_index("col"), 2)
    rank, nb = own.shape
    for side, sk in ((parity, own), (1 - parity, other)):
        two = jnp.concatenate(halves(sk[...]), 0)
        for first, last in blocks_of(nb):
            both = bdot(inverse[side, first:last, :last], two[:, :last], NT)
            high, low = halves(both[:, :rank] + both[:, rank:])
            spread[side, first:last, :] = jnp.concatenate([high, high, low], 1)
        spread_gain[side] = dot3(right_rows[side], sk[...], NT)


def stack3(x):
    high, low = halves(x)
    return jnp.concatenate([high, low, high], 0)


def weight_body(own, other, wp_high, wp_low, offset, gain, spread_gain, weights, offsets, pack):
    parity = lax.rem(lax.axis_index("col"), 2)
    rank = gain.shape[1]
    count = wp_high.shape[0]
    width = wp_high.shape[1]
    for side, middle in ((parity, own), (1 - parity, other)):
        mixed = dot3(middle[:, count : count + rank], middle[:, :count], TN)
        high, low = halves(mixed)
        both = bdot(jnp.concatenate([high, low], 0), wp_high[...])
        weight = both[:rank] + (both[rank:] + bdot(high, wp_low[...]))
        weights[side] = stack3(weight)
        offsets[side] = offset[side] + dot3(spread_gain[side], weight)
    map_offset = offsets[0]
    map_matrix = -gain[0]
    for band in range(1, gain.shape[0]):
        map_offset = offsets[band] - dot3(gain[band], map_offset)
        map_matrix = -dot3(gain[band], map_matrix)
    pack[:, :width] = map_offset
    pack[:, width:] = jnp.concatenate([map_matrix, jnp.zeros_like(map_matrix)], 1)


def compose_body(bit, first, width, near, group, other, near_out, group_out):
    rank = group.shape[0]
    upper = lax.rem(lax.axis_index("row") // bit, 2) == 1

    def chained(then, before):
        matrix = then[:, width : width + rank]
        moved = dot3(matrix, before)
        lanes = lax.broadcasted_iota(jnp.int32, moved.shape, 1)
        return moved + jnp.where(lanes < width, then, 0.0)

    own, far = group[...], other[...]
    group_out[...] = chained(jnp.where(upper, own, far), jnp.where(upper, far, own))
    if first:
        lanes = lax.broadcasted_iota(jnp.int32, own.shape, 1)
        rows = lax.broadcasted_iota(jnp.int32, own.shape, 0)
        identity = jnp.where(lanes == rows + width, 1.0, 0.0).astype(F32)
        near_out[...] = jnp.where(upper, far, identity)
    else:
        near_out[...] = jnp.where(upper, chained(near[...], far), near[...])


def partial_body(base, spread, weights, middle_own, middle_other, slab, out, schur):
    parity = lax.rem(lax.axis_index("col"), 2)
    bands, nb, _ = base.shape
    rank = schur.shape[1]
    count = slab.shape[0]
    for band in range(bands):
        for first, last in blocks_of(nb):
            out[band, first:last, :] = base[band, first:last, :] + bdot(
                spread[band, first:last, :], weights[band]
            )
    for side, middle in ((parity, middle_own), (1 - parity, middle_other)):
        both = bdot(jnp.concatenate(halves(middle[:, :count]), 0), slab[...])
        schur[side] = both[:rank] + both[rank:]


def finish_body(bit, partial, feed, gain, offsets, near, other, carry, solved, states):
    bands, nb, width = partial.shape
    rank = gain.shape[1]
    upper = lax.rem(lax.axis_index("row") // bit, 2) == 1
    prior = carry[...]
    far = dot3(other[:, width : width + rank], prior) + other[:, :width]
    prior = jnp.where(upper, far, prior)
    prior = dot3(near[:, width : width + rank], prior) + near[:, :width]
    for band in range(bands):
        three = stack3(prior)
        prior = offsets[band] - dot3(gain[band], prior)
        states[band] = prior
        for first, last in blocks_of(nb):
            solved[band, first:last, :] = (
                partial[band, first:last, :] - bdot(feed[band, first:last, :], three)
            ).astype(BF16)


def shards(
    tile_left,
    tile_right,
    row_left,
    row_right,
    sketch,
    panel_left,
    panel_right,
    pivot_inverse,
    band_inverse,
    link_left,
    link_right,
    pivot_rhs,
    band_rhs,
    carry_in,
):
    cols = lax.axis_size("col")
    rows = lax.axis_size("row")
    groups = cols // 2
    col = lax.axis_index("col")
    bands, nb, rank = tile_left.shape[1:]
    width = pivot_rhs.shape[1]
    slab = nb // groups
    count = cols * rank

    def swap(x, step):
        return lax.ppermute(x, "col", [(c, c ^ step) for c in range(cols)])

    def row_swap(x, step):
        return lax.ppermute(x, "row", [(r, r ^ step) for r in range(rows)])

    def turned(x):
        return jnp.swapaxes(x, -1, -2)

    row_left_t = turned(row_left[0])
    x_own, x_sent = vmem_call(
        couple_body, [((rank, nb), F32), ((rank, nb + LANES), F32)], name="couple"
    )(turned(tile_left[0]), turned(tile_right[0]), row_left_t, turned(row_right[0]), turned(sketch))
    x_got = swap(x_sent, 1)

    wide = list(vmem_call(widen_body, [((rank, nb // 2), F32)], name="widen")(row_left_t))
    step = 1
    while step < groups:
        wide = wide + [swap(block, 2 * step) for block in wide]
        step *= 2
    wide = wide + [swap(block, 1) for block in wide]
    wide = wide + [row_swap(block, 1) for block in wide]
    (wide,) = vmem_call(
        functools.partial(narrow_body, groups), [((groups, 2, rank, nb), BF16)], name="narrow"
    )(*wide)
    wide = wide.reshape(count, nb)

    pivot_solution = jnp.dot(pivot_inverse, pivot_rhs, preferred_element_type=F32).astype(BF16)
    pulled = bdot(pivot_inverse, pivot_solution, TN)

    def per_band(*shape):
        return pl.BlockSpec((None,) + shape, lambda band: (band, 0, 0))

    base, feed, offset, gain, right_rows = pl.pallas_call(
        band_body,
        grid=(bands,),
        in_specs=[per_band(rank, nb)] * 4
        + [pl.BlockSpec((nb, width), lambda band: (0, 0)), per_band(nb, nb), per_band(nb, width)],
        out_specs=[
            per_band(nb, width),
            per_band(nb, 3 * rank),
            per_band(rank, width),
            per_band(rank, rank),
            per_band(rank, nb),
        ],
        out_shape=[
            jax.ShapeDtypeStruct((bands, nb, width), F32),
            jax.ShapeDtypeStruct((bands, nb, 3 * rank), BF16),
            jax.ShapeDtypeStruct((bands, rank, width), F32),
            jax.ShapeDtypeStruct((bands, rank, rank), F32),
            jax.ShapeDtypeStruct((bands, rank, nb), F32),
        ],
        scratch_shapes=[pltpu.VMEM((nb, width), BF16)],
        compiler_params=pltpu.CompilerParams(vmem_limit_bytes=32 * 2**20),
        cost_estimate=pl.CostEstimate(flops=4 * 10**9, bytes_accessed=10**7, transcendentals=0),
        name="band",
    )(
        turned(panel_right),
        turned(panel_left),
        turned(link_left),
        turned(link_right),
        pulled,
        band_inverse,
        band_rhs,
    )

    pieces = groups if slab % LANES == 0 else 1
    parts = vmem_call(
        functools.partial(sketch_body, pieces),
        [((2 * rank, nb), F32)] + [((rank, nb // pieces), F32)] * pieces,
        [pltpu.VMEM((rank, nb), F32)],
        name="sketch",
    )(x_own, x_sent, x_got)
    x_pair, parts = parts[0], parts[1:]
    if pieces > 1:
        total = parts[0]
        for step in range(1, pieces):
            total = total + swap(parts[step], 2 * step)
        slabs = [total] + [swap(total, 2 * step) for step in range(1, pieces)]
    else:
        members = [list(range(side, cols, 2)) for side in range(2)]
        slabs = [lax.psum(parts[0], "col", axis_index_groups=members)]
    sketched, crossed, gram = vmem_call(
        functools.partial(project_body, pieces),
        [((rank, nb), F32), ((rank, 2 * rank), F32), ((rank, rank), F32)],
        name="project",
    )(x_pair, *slabs)
    crossed_all = [crossed] + [swap(crossed, 2 * step) for step in range(1, groups)]
    sketched_other = swap(sketched, 1)
    (inverse_low,) = vmem_call(factor_body, [((rank, rank), F32)], name="factor")(gram)
    (middle,) = vmem_call(
        functools.partial(scaled_body, groups), [((rank, count + LANES), F32)], name="scaled"
    )(inverse_low, *crossed_all)
    middle_other = swap(middle, 1)

    wp_high, wp_low = vmem_call(
        wide_pulled_body,
        [((count, width), BF16)] * 2,
        flops=10**9,
        name="wide_pulled",
        limit=32,
    )(wide, pulled)
    spread, spread_gain = vmem_call(
        spread_body,
        [((bands, nb, 3 * rank), BF16), ((bands, rank, rank), F32)],
        flops=10**9,
        name="spread",
        limit=32,
    )(band_inverse, right_rows, sketched, sketched_other)
    weights, offsets, pack = vmem_call(
        weight_body,
        [
            ((bands, 3 * rank, width), BF16),
            ((bands, rank, width), F32),
            ((rank, width + LANES), F32),
        ],
        name="weight",
        limit=32,
    )(middle, middle_other, wp_high, wp_low, offset, gain, spread_gain)

    near, group = pack, pack
    step = 1
    while step < rows:
        other = row_swap(group, step)
        if 2 * step < rows:
            near, group = vmem_call(
                functools.partial(compose_body, step, step == 1, width),
                [((rank, width + LANES), F32)] * 2,
                name="compose",
            )(near, group, other)
        step *= 2

    own_slab = lax.dynamic_slice_in_dim(wide, col * (nb // cols), nb // cols, 1)
    partial, schur = vmem_call(
        partial_body,
        [((bands, nb, width), F32), ((bands, rank, nb // cols), F32)],
        flops=10**9,
        name="partial",
        limit=32,
    )(base, spread, weights, middle, middle_other, own_slab)
    solved, states = vmem_call(
        functools.partial(finish_body, rows // 2),
        [((bands, nb, width), BF16), ((bands, rank, width), F32)],
        flops=10**9,
        name="finish",
        limit=32,
    )(partial, feed, gain, offsets, near, other, carry_in)
    return (pivot_solution, turned(schur), solved, states)


def solution(mesh):
    return jax.shard_map(
        shards,
        mesh=mesh,
        in_specs=(
            P("col", "row", None, None),
            P("col", "row", None, None),
            P("col", None, None),
            P("col", None, None),
            P(),
            P("row", None, None),
            P("row", None, None),
            P(),
            P("row", None, None),
            P("row", None, None),
            P("row", None, None),
            P(None, "col"),
            P("row", None, "col"),
            P(None, "col"),
        ),
        out_specs=(
            P(None, "col"),
            P("row", "col", None),
            P("row", None, "col"),
            P("row", None, "col"),
        ),
        check_vma=False,
    )
```

```python
import functools

import jax
import jax.numpy as jnp
from jax import lax
from jax.experimental import pallas as pl
from jax.experimental.pallas import tpu as pltpu
from jax.sharding import PartitionSpec as P

F32 = jnp.float32
BF16 = jnp.bfloat16
LANES = 128
BLOCK = 256
NN = ((1,), (0,))
NT = ((1,), (1,))
TN = ((0,), (0,))


def halves(x):
    high = x.astype(BF16)
    return high, (x - high.astype(F32)).astype(BF16)


def bdot(a, b, dims=NN):
    return lax.dot_general(a, b, (dims, ((), ())), preferred_element_type=F32)


def dot2(a, b, dims=NN):
    high, low = halves(b)
    return bdot(a, high, dims) + bdot(a, low, dims)


def dot3(a, b, dims=NN):
    ah, al = halves(a)
    bh, bl = halves(b)
    return bdot(ah, bh, dims) + (bdot(ah, bl, dims) + bdot(al, bh, dims))


def vmem_call(body, outs, scratch=(), flops=10**7, name=None, limit=16):
    def call(*operands, needs=()):
        count = len(operands)

        def kernel(*refs):
            body(*refs[:count], *refs[count + len(needs) :])

        vmem = pl.BlockSpec(memory_space=pltpu.VMEM)
        return pl.pallas_call(
            kernel,
            in_specs=[vmem] * count + [pl.BlockSpec(memory_space=pl.ANY)] * len(needs),
            out_specs=[vmem] * len(outs),
            out_shape=[jax.ShapeDtypeStruct(s, d) for s, d in outs],
            scratch_shapes=list(scratch),
            compiler_params=pltpu.CompilerParams(vmem_limit_bytes=limit * 2**20),
            cost_estimate=pl.CostEstimate(flops=flops, bytes_accessed=10**6, transcendentals=0),
            name=name,
        )(*operands, *needs)

    return call


def held(x, *needs, weight=0):
    anywhere = pl.BlockSpec(memory_space=pl.ANY)
    return pl.pallas_call(
        lambda *refs: None,
        in_specs=[anywhere] * (1 + len(needs)),
        out_specs=anywhere,
        out_shape=jax.ShapeDtypeStruct(x.shape, x.dtype),
        input_output_aliases={0: 0},
        compiler_params=pltpu.CompilerParams(vmem_limit_bytes=2**20),
        cost_estimate=pl.CostEstimate(flops=weight, bytes_accessed=0, transcendentals=0),
        name="held",
    )(x, *needs)


def blocks_of(extent):
    size = min(BLOCK, extent)
    return [(start, start + size) for start in range(0, extent, size)]


def widen_body(row_left, out):
    half = out.shape[2]
    start = pl.multiple_of(lax.rem(lax.axis_index("row"), 2) * half, half)
    out[0] = row_left[:, pl.ds(start, half)].astype(F32)


def couple_body(
    tl_hbm, tr_hbm, rl_hbm, rr_hbm, sk_hbm, ready, own_hbm, msg_hbm, tl, tr, rl, rr, sk, own, msg, sems
):
    parity = lax.rem(lax.axis_index("col"), 2)
    rank, nb = rl.shape
    copies = [
        pltpu.make_async_copy(source, target, sems.at[index])
        for index, (source, target) in enumerate(
            (
                (tr_hbm, tr),
                (rr_hbm, rr),
                (tl_hbm, tl),
                (rl_hbm, rl),
                (sk_hbm, sk),
                (msg, msg_hbm),
                (own, own_hbm),
            )
        )
    ]
    for copy in copies[:5]:
        copy.start()
    for copy in copies[:5]:
        copy.wait()

    def crossed(band):
        coupling = bdot(tr[band], rr[...], NT)
        high, low = halves(coupling)
        both = bdot(jnp.concatenate([high, low], 1), tl[band], TN)
        return both[:rank] + both[rank:]

    msg[:, :nb] = crossed(1 - parity)
    probe = bdot(rl[...], sk[...], NT)
    msg[:, nb:] = jnp.concatenate([probe, jnp.zeros_like(probe)], 1)
    copies[5].start()
    own[...] = crossed(parity)
    copies[6].start()
    for copy in copies[5:]:
        copy.wait()


def sketch_body(pieces, x_own, sent, got, x_pair, *rest):
    outs, part = rest[:-1], rest[-1]
    col = lax.axis_index("col")
    parity = lax.rem(col, 2)
    place = col // 2
    rank, nb = x_own.shape
    own, other = x_own[...], got[:, :nb]
    probes = jnp.concatenate([sent[:, nb : nb + rank], got[:, nb : nb + rank]], 0)
    part[...] = dot3(probes, jnp.concatenate([own, other], 0), TN)
    x_pair[pl.ds(pl.multiple_of(parity * rank, rank), rank), :] = own
    x_pair[pl.ds(pl.multiple_of((1 - parity) * rank, rank), rank), :] = other
    slab = nb // pieces
    for step in range(pieces):
        start = pl.multiple_of(jnp.bitwise_xor(place, step) * slab, slab) if pieces > 1 else 0
        outs[step][...] = part[:, pl.ds(start, slab)]


def sum_body(*refs):
    total = refs[0][...]
    for part in refs[1:-1]:
        total = total + part[...]
    refs[-1][...] = total


def project_body(pieces, x_pair, *rest):
    slabs, (sk, crossed, gram) = rest[:pieces], rest[pieces:]
    place = lax.axis_index("col") // 2
    slab = slabs[0].shape[1]
    for step in range(pieces):
        start = pl.multiple_of(jnp.bitwise_xor(place, step) * slab, slab) if pieces > 1 else 0
        sk[:, pl.ds(start, slab)] = slabs[step][...]
    whole = sk[...]
    crossed[...] = dot3(whole, x_pair[...], NT)
    gram[...] = lax.dot_general(
        whole, whole, (NT, ((), ())), precision=lax.Precision.HIGHEST, preferred_element_type=F32
    )


def join_body(first, second, out):
    count = first.shape[0]
    out[:count] = first[...]
    out[count:] = second[...]


def narrow_body(order, *refs):
    blocks, out = refs[:-1], refs[-1]
    half = blocks[0].shape[-1]
    parity = lax.rem(lax.axis_index("col"), 2)
    near_start = pl.multiple_of(lax.rem(lax.axis_index("row"), 2) * half, half)
    far_start = pl.multiple_of(half - near_start, half)
    count = len(blocks) // 4
    for quarter, (side, start) in enumerate(
        ((parity, near_start), (1 - parity, near_start), (parity, far_start), (1 - parity, far_start))
    ):
        index = 0
        for chunk in blocks[quarter * count : (quarter + 1) * count]:
            for row in range(chunk.shape[0]):
                out[order[index], side, :, pl.ds(start, half)] = chunk[row].astype(BF16)
                index += 1


def wide_pulled_body(wide, pulled, high_out, low_out):
    pulled_high, pulled_low = halves(pulled[...])
    for first, last in blocks_of(wide.shape[0]):
        rows = wide[first:last, :]
        product = bdot(rows, pulled_high) + bdot(rows, pulled_low)
        high, low = halves(product)
        high_out[first:last, :] = high
        low_out[first:last, :] = low


def factor_body(bands, gram, sketched, *refs):
    right_rows, (inverse_out, upper_out, slope_out) = refs[:bands], refs[bands:]
    parity = lax.rem(lax.axis_index("col"), 2)
    chosen = right_rows[0][...]
    for band in range(1, bands):
        chosen = jnp.where(parity == band, right_rows[band][...], chosen)
    slope_out[...] = dot3(chosen, sketched[...], NT)
    rank = gram.shape[0]
    lanes = 2 * rank
    group = 4
    tile = 8
    rows = lax.broadcasted_iota(jnp.int32, (rank, lanes), 0)
    cols = lax.broadcasted_iota(jnp.int32, (rank, lanes), 1)
    eye = jnp.where(cols == rows + rank, 1.0, 0.0).astype(F32)
    work = jnp.concatenate([gram[...], jnp.zeros((rank, rank), F32)], 1) + eye
    done = []
    scales = []
    for start in range(0, rank, group):
        top = (start // tile) * tile
        if start == top and start:
            done.append(work[:tile])
            work = work[tile:]
        ids = rows[top:]
        height = rank - top
        columns = [
            jnp.broadcast_to(work[:, start + j : start + j + 1], (height, lanes)) for j in range(group)
        ]
        for j in range(group):
            k = start + j
            at = k - top
            pivot = columns[j][at : at + 1, :]
            inverse = 1.0 / pivot
            scales.append(lax.rsqrt(pivot))
            factor = jnp.where(ids > k, columns[j] * inverse, 0.0)
            for later in range(j + 1, group):
                columns[later] = columns[later] - factor * columns[later][at : at + 1, :]
            work = work - factor * work[at : at + 1, :]
    done.append(work)
    whole = jnp.concatenate(done, 0) * jnp.concatenate(scales, 0)
    upper_out[...] = jnp.where(cols >= rows, whole, 0.0)[:, :rank]
    low = whole[:, rank:]
    inverse_out[...] = dot3(low, low, TN)


def scaled_body(groups, inverse, upper, slope, *rest):
    blocks, out = rest[:groups], rest[groups]
    two = jnp.concatenate(halves(inverse[...]), 0)
    rank, width = blocks[0].shape
    for step in range(groups):
        high, low = halves(blocks[step][...])
        both = bdot(two, high)
        out[:, step * width : (step + 1) * width] = both[:rank] + (both[rank:] + bdot(two[:rank], low))
    out[:, groups * width :] = jnp.concatenate([upper[...], slope[...]], 1)


def band_body(band, inverse, rhs, left, right, base, feed, offset, gain, right_rows):
    rank, nb = right.shape[1:]
    for first, last in blocks_of(nb):
        rows = inverse[band, first:last, :last]
        base[first:last, :] = bdot(rows, rhs[band, :last, :])
        both = bdot(rows, left[band, :, :last], NT)
        for side in range(2):
            high, low = halves(both[:, side * rank : (side + 1) * rank])
            feed[side, first:last, :] = jnp.concatenate([high, high, low], 1)
        right_rows[:, first:last] = bdot(right[band, :, first:], inverse[band, first:, first:last])
    two = jnp.concatenate(halves(right_rows[...]), 0)
    both = bdot(two, rhs[band])
    offset[...] = both[:rank] + both[rank:]
    both = bdot(two, left[band], NT)
    gain[...] = both[:rank] + both[rank:]


def spread_body(inverse, own, spread):
    parity = lax.rem(lax.axis_index("col"), 2)
    rank, nb = own.shape
    two = jnp.concatenate(halves(own[...]), 0)
    for first, last in blocks_of(nb):
        both = bdot(inverse[parity, first:last, :last], two[:, :last], NT)
        spread[:, first:last] = (both[:, :rank] + both[:, rank:]).T


def affine_body(bands, *refs):
    offset, gain = refs[:bands], refs[bands : 2 * bands]
    panel_right, pulled, carry, coeffs, plain, constant, matrix_out = refs[2 * bands :]
    rank = carry.shape[0]
    stacked = jnp.concatenate([panel_right[band] for band in range(bands)], 0)
    both = dot2(stacked, pulled[...])
    for band in range(bands):
        coeffs[band] = both[band * rank : (band + 1) * rank]
    constant_now = None
    matrix = None
    for band in range(bands):
        now = offset[band][...] - dot3(gain[band][:, :rank], coeffs[band])
        plain[band] = now
        feed = gain[band][:, rank:]
        constant_now = now - dot3(feed, constant_now) if band else now
        matrix = -dot3(feed, matrix) if band else -feed
    first = lax.axis_index("row") == 0
    constant[...] = constant_now + jnp.where(first, dot3(matrix, carry[...]), 0.0)
    matrix_out[...] = jnp.where(first, 0.0, matrix)


def stack3(x):
    high, low = halves(x)
    return jnp.concatenate([high, low, high], 0)


def weight_body(bands, *refs):
    gain = refs[:bands]
    own, other, wp_high, wp_low, constant, matrix, weights, pack = refs[bands:]
    parity = lax.rem(lax.axis_index("col"), 2)
    rank = own.shape[0]
    count, width = wp_high.shape
    sides = [middle[:, :count] for middle in (own, other)]
    highs, lows = zip(*[halves(side) for side in sides])
    upper = bdot(jnp.concatenate(highs + lows, 0), wp_high[...])
    lower = bdot(jnp.concatenate(highs, 0), wp_low[...])
    own_first = upper[: bands * rank] + (upper[bands * rank :] + lower)
    own_weight, other_weight = own_first[:rank], own_first[rank:]
    ordered = []
    slopes = []
    for band in range(bands):
        ordered.append(jnp.where(parity == band, own_weight, other_weight))
        weights[band] = ordered[band]
        if band:
            slopes = [-dot3(gain[band][:, rank:], slope) for slope in slopes]
        ends = [middle[:, count + rank : count + 2 * rank] for middle in (own, other)]
        slopes.append(jnp.where(parity == band, ends[0], ends[1]))
    pack[:, :width] = constant[...] + dot3(jnp.concatenate(slopes, 1), jnp.concatenate(ordered, 0))
    pack[:, width:] = jnp.concatenate([matrix[...], jnp.zeros((rank, LANES - rank), F32)], 1)


def compose_body(bit, first, width, near, group, other, near_out, group_out):
    rank = group.shape[0]
    upper = lax.rem(lax.axis_index("row") // bit, 2) == 1

    def chained(then, before):
        moved = dot3(then[:, width : width + rank], before)
        lanes = lax.broadcasted_iota(jnp.int32, moved.shape, 1)
        return moved + jnp.where(lanes < width, then, 0.0)

    own, far = group[...], other[...]
    group_out[...] = chained(jnp.where(upper, own, far), jnp.where(upper, far, own))
    if first:
        lanes = lax.broadcasted_iota(jnp.int32, own.shape, 1)
        rows = lax.broadcasted_iota(jnp.int32, own.shape, 0)
        identity = jnp.where(lanes == rows + width, 1.0, 0.0).astype(F32)
        near_out[...] = jnp.where(upper, far, identity)
    else:
        near_out[...] = jnp.where(upper, chained(near[...], far), near[...])


def partial_body(bands, *refs):
    base, feed = refs[:bands], refs[bands : 2 * bands]
    own, other, weights, coeffs, plain, middle_own, middle_other, slab, out, offsets, schur = refs[2 * bands :]
    parity = lax.rem(lax.axis_index("col"), 2)
    nb = out.shape[1]
    rank = schur.shape[1]
    count, extent = slab.shape
    for band in range(bands):
        weight = weights[band]
        weight_three = stack3(weight)
        coeffs_three = stack3(coeffs[band])
        high, low = halves(jnp.where(parity == band, own[...], other[...]))
        spread = jnp.concatenate([high, high, low], 0)
        for first, last in blocks_of(nb):
            out[band, first:last, :] = (
                base[band][first:last, :]
                + bdot(spread[:, first:last], weight_three, TN)
                - bdot(feed[band][0, first:last, :], coeffs_three)
            )
        slope = jnp.where(
            parity == band,
            middle_own[:, count + rank : count + 2 * rank],
            middle_other[:, count + rank : count + 2 * rank],
        )
        offsets[band] = plain[band] + dot3(slope, weight)
    width = schur.shape[2]
    if extent == width:
        columns = slab[...]
    else:
        start = pl.multiple_of(lax.axis_index("col") * width, width)
        columns = slab[:, pl.ds(start, width)]
    for side, middle in ((parity, middle_own), (1 - parity, middle_other)):
        basis_side = dot3(middle[:, count : count + rank], middle[:, :count])
        both = bdot(jnp.concatenate(halves(basis_side), 0), columns)
        schur[side] = both[:rank] + both[rank:]


def finish_body(bands, bit, *refs):
    feed, gain = refs[:bands], refs[bands : 2 * bands]
    partial, offsets, near, other, carry, solved_hbm, states, solved, sems = refs[2 * bands :]
    _, nb, width = partial.shape
    rank = carry.shape[0]
    upper = lax.rem(lax.axis_index("row") // bit, 2) == 1
    prior = jnp.where(upper, other[...], carry[...])
    prior = dot3(near[:, width : width + rank], prior) + near[:, :width]
    threes = []
    for band in range(bands):
        threes.append(stack3(prior))
        prior = offsets[band] - dot3(gain[band][:, rank:], prior)
        states[band] = prior
    copies = []
    for band in range(bands):
        for first, last in blocks_of(nb):
            solved[band, first:last, :] = (
                partial[band, first:last, :] - bdot(feed[band][1, first:last, :], threes[band])
            ).astype(BF16)
            copy = pltpu.make_async_copy(
                solved.at[band, first:last, :],
                solved_hbm.at[band, first:last, :],
                sems.at[len(copies)],
            )
            copy.start()
            copies.append(copy)
    for copy in copies:
        copy.wait()


def shards(
    tile_left,
    tile_right,
    row_left,
    row_right,
    sketch,
    panel_left,
    panel_right,
    pivot_inverse,
    band_inverse,
    link_left,
    link_right,
    pivot_rhs,
    band_rhs,
    carry_in,
):
    cols = lax.axis_size("col")
    rows = lax.axis_size("row")
    groups = cols // 2
    col = lax.axis_index("col")
    bands, nb, rank = tile_left.shape[1:]
    width = pivot_rhs.shape[1]
    slab = nb // groups
    count = cols * rank

    def swap(x, step):
        return lax.ppermute(x, "col", [(c, c ^ step) for c in range(cols)])

    def row_swap(x, step):
        return lax.ppermute(x, "row", [(r, r ^ step) for r in range(rows)])

    def turned(x):
        return jnp.swapaxes(x, -1, -2)

    def joined(first, second, *needs):
        shape = (2 * first.shape[0],) + first.shape[1:]
        return vmem_call(join_body, [(shape, F32)], name="join")(first, second, needs=needs)[0]

    row_left_t = turned(row_left[0])
    (wide,) = vmem_call(widen_body, [((1, rank, nb // 2), F32)], name="widen")(row_left_t)
    order = [0]
    reach = groups // 2
    def hbm(count):
        return [pl.BlockSpec(memory_space=pltpu.HBM)] * count

    x_own, x_sent = pl.pallas_call(
        couple_body,
        in_specs=hbm(5) + [pl.BlockSpec(memory_space=pl.ANY)],
        out_specs=hbm(2),
        out_shape=[
            jax.ShapeDtypeStruct((rank, nb), F32),
            jax.ShapeDtypeStruct((rank, nb + LANES), F32),
        ],
        scratch_shapes=[pltpu.VMEM((bands, rank, nb), BF16)] * 2
        + [pltpu.VMEM((rank, nb), BF16)] * 3
        + [
            pltpu.VMEM((rank, nb), F32),
            pltpu.VMEM((rank, nb + LANES), F32),
            pltpu.SemaphoreType.DMA((7,)),
        ],
        compiler_params=pltpu.CompilerParams(vmem_limit_bytes=60 * 2**20),
        name="couple",
    )(
        turned(tile_left[0]),
        turned(tile_right[0]),
        row_left_t,
        turned(row_right[0]),
        turned(sketch),
        wide,
    )
    x_got = swap(x_sent, 1)

    pivot_solution = jnp.dot(pivot_inverse, pivot_rhs, preferred_element_type=F32).astype(BF16)
    pulled = bdot(pivot_inverse, pivot_solution, TN)

    def one_band(band, *needs):
        shapes = [(nb, width), (2, nb, 3 * rank), (rank, width), (rank, 2 * rank), (rank, nb)]
        return vmem_call(
            functools.partial(band_body, band),
            [(shape, BF16 if index == 1 else F32) for index, shape in enumerate(shapes)],
            flops=2 * 10**9,
            name="band",
        )(band_inverse, band_rhs, left_t, right_t, needs=needs)

    if reach:
        wide = joined(wide, swap(wide, 2 * reach))
        order = order + [place ^ reach for place in order]
        reach //= 2
    pieces = groups if slab % LANES == 0 else 1
    parts = vmem_call(
        functools.partial(sketch_body, pieces),
        [((2 * rank, nb), F32)] + [((rank, nb // pieces), F32)] * pieces,
        [pltpu.VMEM((rank, nb), F32)],
        name="sketch",
    )(x_own, x_sent, x_got, needs=(pulled, wide))
    x_pair, parts = parts[0], parts[1:]

    left_t = jnp.concatenate([turned(panel_left), turned(link_left)], 1)
    right_t = turned(link_right)
    whole_bands = []
    for band in range(bands):
        whole_bands.append(one_band(band, x_pair, *(last[-1] for last in whole_bands[-1:])))
    bases, feeds, offsets_in, gains, right_rows = zip(*whole_bands)
    coeffs, plain, constant, matrix = vmem_call(
        functools.partial(affine_body, bands),
        [((bands, rank, width), F32)] * 2 + [((rank, width), F32), ((rank, rank), F32)],
        name="affine",
    )(*offsets_in, *gains, turned(panel_right), pulled, carry_in)

    if pieces > 1:
        (total,) = vmem_call(sum_body, [((rank, slab), F32)], name="sum")(
            parts[0],
            *[swap(parts[step], 2 * step) for step in range(1, pieces)],
            needs=(wide, matrix),
        )
        slabs = [total] + [swap(total, 2 * step) for step in range(1, pieces)]
    else:
        members = [list(range(side, cols, 2)) for side in range(2)]
        total = lax.psum(parts[0], "col", axis_index_groups=members)
        slabs = [total]
    while reach:
        wide = joined(wide, swap(wide, 2 * reach), total)
        order = order + [place ^ reach for place in order]
        reach //= 2
    wide_other = held(swap(wide, 1), weight=0)
    sketched, crossed, gram = vmem_call(
        functools.partial(project_body, pieces),
        [((rank, nb), F32), ((rank, 2 * rank), F32), ((rank, rank), F32)],
        name="project",
    )(x_pair, *slabs)
    crossed_all = [crossed] + [swap(crossed, 2 * step) for step in range(1, groups)]
    inverse_gram, upper, slope = vmem_call(
        functools.partial(factor_body, bands), [((rank, rank), F32)] * 3, flops=3 * 10**10, name="factor"
    )(gram, sketched, *right_rows)
    (middle,) = vmem_call(
        functools.partial(scaled_body, groups), [((rank, count + LANES), F32)], name="scaled"
    )(inverse_gram, upper, slope, *crossed_all)
    middle_other = held(swap(middle, 1), weight=3 * 10**10)
    (spread,) = vmem_call(spread_body, [((rank, nb), F32)], name="spread")(
        band_inverse, sketched, needs=(middle, wide_other)
    )
    spread_other = swap(spread, 1)

    (wide,) = vmem_call(
        functools.partial(narrow_body, order), [((groups, 2, rank, nb), BF16)], name="narrow"
    )(wide, wide_other, row_swap(wide, 1), row_swap(wide_other, 1))
    wide = wide.reshape(count, nb)
    wp_high, wp_low = vmem_call(
        wide_pulled_body, [((count, width), BF16)] * 2, name="wide_pulled"
    )(wide, pulled)
    weights, pack = vmem_call(
        functools.partial(weight_body, bands),
        [((bands, rank, width), F32), ((rank, width + LANES), F32)],
        name="weight",
    )(*gains, middle, middle_other, wp_high, wp_low, constant, matrix)

    near, group = pack, pack
    step = 1
    while 2 * step < rows:
        near, group = vmem_call(
            functools.partial(compose_body, step, step == 1, width),
            [((rank, width + LANES), F32)] * 2,
            name="compose",
        )(near, group, row_swap(group, step))
        step *= 2
    arrived = row_swap(group[:, :width], step)

    own_slab = wide
    if (nb // cols) % LANES:
        own_slab = lax.dynamic_slice_in_dim(wide, col * (nb // cols), nb // cols, 1)
    partial, offsets, schur = vmem_call(
        functools.partial(partial_body, bands),
        [
            ((bands, nb, width), F32),
            ((bands, rank, width), F32),
            ((bands, rank, nb // cols), F32),
        ],
        flops=10**9,
        name="partial",
    )(
        *bases,
        *feeds,
        spread,
        spread_other,
        weights,
        coeffs,
        plain,
        middle,
        middle_other,
        own_slab,
        needs=(group,),
    )
    vmem = pl.BlockSpec(memory_space=pltpu.VMEM)
    solved, states = pl.pallas_call(
        functools.partial(finish_body, bands, step),
        in_specs=[vmem] * (2 * bands + 5),
        out_specs=[pl.BlockSpec(memory_space=pltpu.HBM), vmem],
        out_shape=[
            jax.ShapeDtypeStruct((bands, nb, width), BF16),
            jax.ShapeDtypeStruct((bands, rank, width), F32),
        ],
        scratch_shapes=[
            pltpu.VMEM((bands, nb, width), BF16),
            pltpu.SemaphoreType.DMA((bands * len(blocks_of(nb)),)),
        ],
        compiler_params=pltpu.CompilerParams(vmem_limit_bytes=16 * 2**20),
        cost_estimate=pl.CostEstimate(flops=10**9, bytes_accessed=10**6, transcendentals=0),
        name="finish",
    )(*feeds, *gains, partial, offsets, near, arrived, carry_in)
    return (pivot_solution, turned(schur), solved, states)


def solution(mesh):
    return jax.shard_map(
        shards,
        mesh=mesh,
        in_specs=(
            P("col", "row", None, None),
            P("col", "row", None, None),
            P("col", None, None),
            P("col", None, None),
            P(),
            P("row", None, None),
            P("row", None, None),
            P(),
            P("row", None, None),
            P("row", None, None),
            P("row", None, None),
            P(None, "col"),
            P("row", None, "col"),
            P(None, "col"),
        ),
        out_specs=(
            P(None, "col"),
            P("row", "col", None),
            P("row", None, "col"),
            P("row", None, "col"),
        ),
        check_vma=False,
    )
```

```python
import functools

import jax
import jax.numpy as jnp
from jax import lax
from jax.experimental import pallas as pl
from jax.experimental.pallas import tpu as pltpu
from jax.sharding import PartitionSpec as P

F32 = jnp.float32
BF16 = jnp.bfloat16
LANES = 128
BLOCK = 256
NN = ((1,), (0,))
NT = ((1,), (1,))
TN = ((0,), (0,))


def halves(x):
    high = x.astype(BF16)
    return high, (x - high.astype(F32)).astype(BF16)


def bdot(a, b, dims=NN):
    return lax.dot_general(a, b, (dims, ((), ())), preferred_element_type=F32)


def dot2(a, b, dims=NN):
    high, low = halves(b)
    return bdot(a, high, dims) + bdot(a, low, dims)


def dot3(a, b, dims=NN):
    ah, al = halves(a)
    bh, bl = halves(b)
    return bdot(ah, bh, dims) + (bdot(ah, bl, dims) + bdot(al, bh, dims))


def vmem_call(body, outs, scratch=(), flops=10**7, name=None, limit=16):
    def call(*operands, needs=()):
        count = len(operands)

        def kernel(*refs):
            body(*refs[:count], *refs[count + len(needs) :])

        vmem = pl.BlockSpec(memory_space=pltpu.VMEM)
        return pl.pallas_call(
            kernel,
            in_specs=[vmem] * count + [pl.BlockSpec(memory_space=pl.ANY)] * len(needs),
            out_specs=[vmem] * len(outs),
            out_shape=[jax.ShapeDtypeStruct(s, d) for s, d in outs],
            scratch_shapes=list(scratch),
            compiler_params=pltpu.CompilerParams(vmem_limit_bytes=limit * 2**20),
            cost_estimate=pl.CostEstimate(flops=flops, bytes_accessed=10**6, transcendentals=0),
            name=name,
        )(*operands, *needs)

    return call


def held(x, *needs, weight=0):
    anywhere = pl.BlockSpec(memory_space=pl.ANY)
    return pl.pallas_call(
        lambda *refs: None,
        in_specs=[anywhere] * (1 + len(needs)),
        out_specs=anywhere,
        out_shape=jax.ShapeDtypeStruct(x.shape, x.dtype),
        input_output_aliases={0: 0},
        compiler_params=pltpu.CompilerParams(vmem_limit_bytes=2**20),
        cost_estimate=pl.CostEstimate(flops=weight, bytes_accessed=0, transcendentals=0),
        name="held",
    )(x, *needs)


def blocks_of(extent):
    size = min(BLOCK, extent)
    return [(start, start + size) for start in range(0, extent, size)]


def widen_body(row_left, out):
    half = out.shape[2]
    start = pl.multiple_of(lax.rem(lax.axis_index("row"), 2) * half, half)
    out[0] = row_left[:, pl.ds(start, half)].astype(F32)


def couple_body(
    tl_hbm, tr_hbm, rl_hbm, rr_hbm, sk_hbm, ready, own_hbm, msg_hbm, tl, tr, rl, rr, sk, own, msg, sems
):
    parity = lax.rem(lax.axis_index("col"), 2)
    rank, nb = rl.shape
    copies = [
        pltpu.make_async_copy(source, target, sems.at[index])
        for index, (source, target) in enumerate(
            (
                (tr_hbm, tr),
                (rr_hbm, rr),
                (tl_hbm, tl),
                (rl_hbm, rl),
                (sk_hbm, sk),
                (msg, msg_hbm),
                (own, own_hbm),
            )
        )
    ]
    for copy in copies[:5]:
        copy.start()
    for copy in copies[:5]:
        copy.wait()

    def crossed(band):
        coupling = bdot(tr[band], rr[...], NT)
        high, low = halves(coupling)
        both = bdot(jnp.concatenate([high, low], 1), tl[band], TN)
        return both[:rank] + both[rank:]

    msg[:, :nb] = crossed(1 - parity)
    probe = bdot(rl[...], sk[...], NT)
    msg[:, nb:] = jnp.concatenate([probe, jnp.zeros_like(probe)], 1)
    copies[5].start()
    own[...] = crossed(parity)
    copies[6].start()
    for copy in copies[5:]:
        copy.wait()


def sketch_body(pieces, x_own, sent, got, x_pair, *rest):
    outs, part = rest[:-1], rest[-1]
    col = lax.axis_index("col")
    parity = lax.rem(col, 2)
    place = col // 2
    rank, nb = x_own.shape
    own, other = x_own[...], got[:, :nb]
    probes = jnp.concatenate([sent[:, nb : nb + rank], got[:, nb : nb + rank]], 0)
    part[...] = dot3(probes, jnp.concatenate([own, other], 0), TN)
    x_pair[pl.ds(pl.multiple_of(parity * rank, rank), rank), :] = own
    x_pair[pl.ds(pl.multiple_of((1 - parity) * rank, rank), rank), :] = other
    slab = nb // pieces
    for step in range(pieces):
        start = pl.multiple_of(jnp.bitwise_xor(place, step) * slab, slab) if pieces > 1 else 0
        outs[step][...] = part[:, pl.ds(start, slab)]


def sum_body(*refs):
    total = refs[0][...]
    for part in refs[1:-1]:
        total = total + part[...]
    refs[-1][...] = total


def project_body(pieces, x_pair, *rest):
    slabs, (sk, crossed, gram) = rest[:pieces], rest[pieces:]
    place = lax.axis_index("col") // 2
    slab = slabs[0].shape[1]
    for step in range(pieces):
        start = pl.multiple_of(jnp.bitwise_xor(place, step) * slab, slab) if pieces > 1 else 0
        sk[:, pl.ds(start, slab)] = slabs[step][...]
    whole = sk[...]
    crossed[...] = dot3(whole, x_pair[...], NT)
    gram[...] = lax.dot_general(
        whole, whole, (NT, ((), ())), precision=lax.Precision.HIGHEST, preferred_element_type=F32
    )


def join_body(first, second, out):
    count = first.shape[0]
    out[:count] = first[...]
    out[count:] = second[...]


def narrow_body(order, *refs):
    blocks, out = refs[:-1], refs[-1]
    half = blocks[0].shape[-1]
    parity = lax.rem(lax.axis_index("col"), 2)
    near_start = pl.multiple_of(lax.rem(lax.axis_index("row"), 2) * half, half)
    far_start = pl.multiple_of(half - near_start, half)
    count = len(blocks) // 4
    for quarter, (side, start) in enumerate(
        ((parity, near_start), (1 - parity, near_start), (parity, far_start), (1 - parity, far_start))
    ):
        index = 0
        for chunk in blocks[quarter * count : (quarter + 1) * count]:
            for row in range(chunk.shape[0]):
                out[order[index], side, :, pl.ds(start, half)] = chunk[row].astype(BF16)
                index += 1


def wide_pulled_body(wide, pulled, high_out, low_out):
    pulled_high, pulled_low = halves(pulled[...])
    for first, last in blocks_of(wide.shape[0]):
        rows = wide[first:last, :]
        product = bdot(rows, pulled_high) + bdot(rows, pulled_low)
        high, low = halves(product)
        high_out[first:last, :] = high
        low_out[first:last, :] = low


def factor_body(bands, gram, sketched, *refs):
    right_rows, (inverse_out, upper_out, slope_out) = refs[:bands], refs[bands:]
    parity = lax.rem(lax.axis_index("col"), 2)
    chosen = right_rows[0][...]
    for band in range(1, bands):
        chosen = jnp.where(parity == band, right_rows[band][...], chosen)
    slope_out[...] = dot3(chosen, sketched[...], NT)
    rank = gram.shape[0]
    lanes = 2 * rank
    group = 4
    tile = 8
    rows = lax.broadcasted_iota(jnp.int32, (rank, lanes), 0)
    cols = lax.broadcasted_iota(jnp.int32, (rank, lanes), 1)
    eye = jnp.where(cols == rows + rank, 1.0, 0.0).astype(F32)
    work = jnp.concatenate([gram[...], jnp.zeros((rank, rank), F32)], 1) + eye
    done = []
    scales = []
    for start in range(0, rank, group):
        top = (start // tile) * tile
        if start == top and start:
            done.append(work[:tile])
            work = work[tile:]
        ids = rows[top:]
        height = rank - top
        columns = [
            jnp.broadcast_to(work[:, start + j : start + j + 1], (height, lanes)) for j in range(group)
        ]
        for j in range(group):
            k = start + j
            at = k - top
            pivot = columns[j][at : at + 1, :]
            inverse = 1.0 / pivot
            scales.append(lax.rsqrt(pivot))
            factor = jnp.where(ids > k, columns[j] * inverse, 0.0)
            for later in range(j + 1, group):
                columns[later] = columns[later] - factor * columns[later][at : at + 1, :]
            work = work - factor * work[at : at + 1, :]
    done.append(work)
    whole = jnp.concatenate(done, 0) * jnp.concatenate(scales, 0)
    upper_out[...] = jnp.where(cols >= rows, whole, 0.0)[:, :rank]
    low = whole[:, rank:]
    inverse_out[...] = dot3(low, low, TN)


def scaled_body(groups, inverse, upper, slope, *rest):
    blocks, out = rest[:groups], rest[groups]
    two = jnp.concatenate(halves(inverse[...]), 0)
    rank, width = blocks[0].shape
    for step in range(groups):
        high, low = halves(blocks[step][...])
        both = bdot(two, high)
        out[:, step * width : (step + 1) * width] = both[:rank] + (both[rank:] + bdot(two[:rank], low))
    out[:, groups * width :] = jnp.concatenate([upper[...], slope[...]], 1)


def band_body(band, inverse, rhs, left, right, base, feed, offset, gain, right_rows):
    rank, nb = right.shape[1:]
    for first, last in blocks_of(nb):
        rows = inverse[band, first:last, :last]
        base[first:last, :] = bdot(rows, rhs[band, :last, :])
        both = bdot(rows, left[band, :, :last], NT)
        for side in range(2):
            high, low = halves(both[:, side * rank : (side + 1) * rank])
            feed[side, first:last, :] = jnp.concatenate([high, high, low], 1)
        right_rows[:, first:last] = bdot(right[band, :, first:], inverse[band, first:, first:last])
    two = jnp.concatenate(halves(right_rows[...]), 0)
    both = bdot(two, rhs[band])
    offset[...] = both[:rank] + both[rank:]
    both = bdot(two, left[band], NT)
    gain[...] = both[:rank] + both[rank:]


def spread_body(inverse, own, spread):
    parity = lax.rem(lax.axis_index("col"), 2)
    rank, nb = own.shape
    two = jnp.concatenate(halves(own[...]), 0)
    for first, last in blocks_of(nb):
        both = bdot(inverse[parity, first:last, :last], two[:, :last], NT)
        spread[:, first:last] = (both[:, :rank] + both[:, rank:]).T


def affine_body(bands, *refs):
    offset, gain = refs[:bands], refs[bands : 2 * bands]
    panel_right, pulled, carry, coeffs, plain, constant, matrix_out = refs[2 * bands :]
    rank = carry.shape[0]
    stacked = jnp.concatenate([panel_right[band] for band in range(bands)], 0)
    both = dot2(stacked, pulled[...])
    for band in range(bands):
        coeffs[band] = both[band * rank : (band + 1) * rank]
    constant_now = None
    matrix = None
    for band in range(bands):
        now = offset[band][...] - dot3(gain[band][:, :rank], coeffs[band])
        plain[band] = now
        feed = gain[band][:, rank:]
        constant_now = now - dot3(feed, constant_now) if band else now
        matrix = -dot3(feed, matrix) if band else -feed
    first = lax.axis_index("row") == 0
    constant[...] = constant_now + jnp.where(first, dot3(matrix, carry[...]), 0.0)
    matrix_out[...] = jnp.where(first, 0.0, matrix)


def stack3(x):
    high, low = halves(x)
    return jnp.concatenate([high, low, high], 0)


def weight_body(bands, *refs):
    gain = refs[:bands]
    own, other, wp_high, wp_low, constant, matrix, weights, pack = refs[bands:]
    parity = lax.rem(lax.axis_index("col"), 2)
    rank = own.shape[0]
    count, width = wp_high.shape
    sides = [middle[:, :count] for middle in (own, other)]
    highs, lows = zip(*[halves(side) for side in sides])
    upper = bdot(jnp.concatenate(highs + lows, 0), wp_high[...])
    lower = bdot(jnp.concatenate(highs, 0), wp_low[...])
    own_first = upper[: bands * rank] + (upper[bands * rank :] + lower)
    own_weight, other_weight = own_first[:rank], own_first[rank:]
    ordered = []
    slopes = []
    for band in range(bands):
        ordered.append(jnp.where(parity == band, own_weight, other_weight))
        weights[band] = ordered[band]
        if band:
            slopes = [-dot3(gain[band][:, rank:], slope) for slope in slopes]
        ends = [middle[:, count + rank : count + 2 * rank] for middle in (own, other)]
        slopes.append(jnp.where(parity == band, ends[0], ends[1]))
    pack[:, :width] = constant[...] + dot3(jnp.concatenate(slopes, 1), jnp.concatenate(ordered, 0))
    pack[:, width:] = jnp.concatenate([matrix[...], jnp.zeros((rank, LANES - rank), F32)], 1)


def compose_body(bit, first, width, near, group, other, near_out, group_out):
    rank = group.shape[0]
    upper = lax.rem(lax.axis_index("row") // bit, 2) == 1

    def chained(then, before):
        moved = dot3(then[:, width : width + rank], before)
        lanes = lax.broadcasted_iota(jnp.int32, moved.shape, 1)
        return moved + jnp.where(lanes < width, then, 0.0)

    own, far = group[...], other[...]
    group_out[...] = chained(jnp.where(upper, own, far), jnp.where(upper, far, own))
    if first:
        lanes = lax.broadcasted_iota(jnp.int32, own.shape, 1)
        rows = lax.broadcasted_iota(jnp.int32, own.shape, 0)
        identity = jnp.where(lanes == rows + width, 1.0, 0.0).astype(F32)
        near_out[...] = jnp.where(upper, far, identity)
    else:
        near_out[...] = jnp.where(upper, chained(near[...], far), near[...])


def partial_body(bands, *refs):
    base, feed = refs[:bands], refs[bands : 2 * bands]
    own, other, weights, coeffs, plain, middle_own, middle_other, slab, out, offsets, schur = refs[2 * bands :]
    parity = lax.rem(lax.axis_index("col"), 2)
    nb = out.shape[1]
    rank = schur.shape[1]
    count, extent = slab.shape
    for band in range(bands):
        weight = weights[band]
        weight_three = stack3(weight)
        coeffs_three = stack3(coeffs[band])
        high, low = halves(jnp.where(parity == band, own[...], other[...]))
        spread = jnp.concatenate([high, high, low], 0)
        for first, last in blocks_of(nb):
            out[band, first:last, :] = (
                base[band][first:last, :]
                + bdot(spread[:, first:last], weight_three, TN)
                - bdot(feed[band][0, first:last, :], coeffs_three)
            )
        slope = jnp.where(
            parity == band,
            middle_own[:, count + rank : count + 2 * rank],
            middle_other[:, count + rank : count + 2 * rank],
        )
        offsets[band] = plain[band] + dot3(slope, weight)
    width = schur.shape[2]
    if extent == width:
        columns = slab[...]
    else:
        start = pl.multiple_of(lax.axis_index("col") * width, width)
        columns = slab[:, pl.ds(start, width)]
    for side, middle in ((parity, middle_own), (1 - parity, middle_other)):
        basis_side = dot3(middle[:, count : count + rank], middle[:, :count])
        both = bdot(jnp.concatenate(halves(basis_side), 0), columns)
        schur[side] = both[:rank] + both[rank:]


def finish_body(bands, bit, *refs):
    feed, gain = refs[:bands], refs[bands : 2 * bands]
    partial, offsets, near, other, carry, solved_hbm, states, solved, sems = refs[2 * bands :]
    _, nb, width = partial.shape
    rank = carry.shape[0]
    upper = lax.rem(lax.axis_index("row") // bit, 2) == 1
    prior = jnp.where(upper, other[...], carry[...])
    prior = dot3(near[:, width : width + rank], prior) + near[:, :width]
    copies = []
    for band in range(bands):
        three = stack3(prior)
        for first, last in blocks_of(nb):
            solved[band, first:last, :] = (
                partial[band, first:last, :] - bdot(feed[band][1, first:last, :], three)
            ).astype(BF16)
            copy = pltpu.make_async_copy(
                solved.at[band, first:last, :],
                solved_hbm.at[band, first:last, :],
                sems.at[len(copies)],
            )
            copy.start()
            copies.append(copy)
        prior = offsets[band] - dot3(gain[band][:, rank:], prior)
        states[band] = prior
    for copy in copies:
        copy.wait()


def shards(
    tile_left,
    tile_right,
    row_left,
    row_right,
    sketch,
    panel_left,
    panel_right,
    pivot_inverse,
    band_inverse,
    link_left,
    link_right,
    pivot_rhs,
    band_rhs,
    carry_in,
):
    cols = lax.axis_size("col")
    rows = lax.axis_size("row")
    groups = cols // 2
    col = lax.axis_index("col")
    bands, nb, rank = tile_left.shape[1:]
    width = pivot_rhs.shape[1]
    slab = nb // groups
    count = cols * rank

    def swap(x, step):
        return lax.ppermute(x, "col", [(c, c ^ step) for c in range(cols)])

    def row_swap(x, step):
        return lax.ppermute(x, "row", [(r, r ^ step) for r in range(rows)])

    def turned(x):
        return jnp.swapaxes(x, -1, -2)

    def joined(first, second, *needs):
        shape = (2 * first.shape[0],) + first.shape[1:]
        return vmem_call(join_body, [(shape, F32)], name="join")(first, second, needs=needs)[0]

    row_left_t = turned(row_left[0])
    (wide,) = vmem_call(widen_body, [((1, rank, nb // 2), F32)], name="widen")(row_left_t)
    order = [0]
    reach = groups // 2
    def hbm(count):
        return [pl.BlockSpec(memory_space=pltpu.HBM)] * count

    x_own, x_sent = pl.pallas_call(
        couple_body,
        in_specs=hbm(5) + [pl.BlockSpec(memory_space=pl.ANY)],
        out_specs=hbm(2),
        out_shape=[
            jax.ShapeDtypeStruct((rank, nb), F32),
            jax.ShapeDtypeStruct((rank, nb + LANES), F32),
        ],
        scratch_shapes=[pltpu.VMEM((bands, rank, nb), BF16)] * 2
        + [pltpu.VMEM((rank, nb), BF16)] * 3
        + [
            pltpu.VMEM((rank, nb), F32),
            pltpu.VMEM((rank, nb + LANES), F32),
            pltpu.SemaphoreType.DMA((7,)),
        ],
        compiler_params=pltpu.CompilerParams(vmem_limit_bytes=60 * 2**20),
        name="couple",
    )(
        turned(tile_left[0]),
        turned(tile_right[0]),
        row_left_t,
        turned(row_right[0]),
        turned(sketch),
        wide,
    )
    x_got = swap(x_sent, 1)

    pivot_solution = jnp.dot(pivot_inverse, pivot_rhs, preferred_element_type=F32).astype(BF16)
    pulled = bdot(pivot_inverse, pivot_solution, TN)

    def one_band(band, *needs):
        shapes = [(nb, width), (2, nb, 3 * rank), (rank, width), (rank, 2 * rank), (rank, nb)]
        return vmem_call(
            functools.partial(band_body, band),
            [(shape, BF16 if index == 1 else F32) for index, shape in enumerate(shapes)],
            flops=2 * 10**9,
            name="band",
        )(band_inverse, band_rhs, left_t, right_t, needs=needs)

    if reach:
        wide = joined(wide, swap(wide, 2 * reach))
        order = order + [place ^ reach for place in order]
        reach //= 2
    pieces = groups if slab % LANES == 0 else 1
    parts = vmem_call(
        functools.partial(sketch_body, pieces),
        [((2 * rank, nb), F32)] + [((rank, nb // pieces), F32)] * pieces,
        [pltpu.VMEM((rank, nb), F32)],
        name="sketch",
    )(x_own, x_sent, x_got, needs=(pulled, wide))
    x_pair, parts = parts[0], parts[1:]

    left_t = jnp.concatenate([turned(panel_left), turned(link_left)], 1)
    right_t = turned(link_right)
    whole_bands = []
    for band in range(bands):
        whole_bands.append(one_band(band, x_pair, *(last[-1] for last in whole_bands[-1:])))
    bases, feeds, offsets_in, gains, right_rows = zip(*whole_bands)
    coeffs, plain, constant, matrix = vmem_call(
        functools.partial(affine_body, bands),
        [((bands, rank, width), F32)] * 2 + [((rank, width), F32), ((rank, rank), F32)],
        name="affine",
    )(*offsets_in, *gains, turned(panel_right), pulled, carry_in)

    if pieces > 1:
        (total,) = vmem_call(sum_body, [((rank, slab), F32)], name="sum")(
            parts[0],
            *[swap(parts[step], 2 * step) for step in reversed(range(1, pieces))],
            needs=(wide, matrix),
        )
        slabs = [total] + [swap(total, 2 * step) for step in reversed(range(1, pieces))][::-1]
    else:
        members = [list(range(side, cols, 2)) for side in range(2)]
        total = lax.psum(parts[0], "col", axis_index_groups=members)
        slabs = [total]
    while reach:
        wide = joined(wide, swap(wide, 2 * reach), total)
        order = order + [place ^ reach for place in order]
        reach //= 2
    wide_other = held(swap(wide, 1), weight=0)
    sketched, crossed, gram = vmem_call(
        functools.partial(project_body, pieces),
        [((rank, nb), F32), ((rank, 2 * rank), F32), ((rank, rank), F32)],
        name="project",
    )(x_pair, *slabs)
    crossed_all = [crossed] + [swap(crossed, 2 * step) for step in reversed(range(1, groups))][::-1]
    inverse_gram, upper, slope = vmem_call(
        functools.partial(factor_body, bands), [((rank, rank), F32)] * 3, flops=3 * 10**10, name="factor"
    )(gram, sketched, *right_rows)
    (middle,) = vmem_call(
        functools.partial(scaled_body, groups), [((rank, count + LANES), F32)], name="scaled"
    )(inverse_gram, upper, slope, *crossed_all)
    middle_other = held(swap(middle, 1), weight=3 * 10**10)
    (spread,) = vmem_call(spread_body, [((rank, nb), F32)], name="spread")(
        band_inverse, sketched, needs=(middle, wide_other)
    )
    spread_other = swap(spread, 1)

    (wide,) = vmem_call(
        functools.partial(narrow_body, order), [((groups, 2, rank, nb), BF16)], name="narrow"
    )(wide, wide_other, row_swap(wide, 1), row_swap(wide_other, 1))
    wide = wide.reshape(count, nb)
    wp_high, wp_low = vmem_call(
        wide_pulled_body, [((count, width), BF16)] * 2, name="wide_pulled"
    )(wide, pulled)
    weights, pack = vmem_call(
        functools.partial(weight_body, bands),
        [((bands, rank, width), F32), ((rank, width + LANES), F32)],
        name="weight",
    )(*gains, middle, middle_other, wp_high, wp_low, constant, matrix)

    near, group = pack, pack
    step = 1
    while 2 * step < rows:
        near, group = vmem_call(
            functools.partial(compose_body, step, step == 1, width),
            [((rank, width + LANES), F32)] * 2,
            name="compose",
        )(near, group, row_swap(group, step))
        step *= 2
    arrived = row_swap(group[:, :width], step)

    own_slab = wide
    if (nb // cols) % LANES:
        own_slab = lax.dynamic_slice_in_dim(wide, col * (nb // cols), nb // cols, 1)
    partial, offsets, schur = vmem_call(
        functools.partial(partial_body, bands),
        [
            ((bands, nb, width), F32),
            ((bands, rank, width), F32),
            ((bands, rank, nb // cols), F32),
        ],
        flops=10**9,
        name="partial",
    )(
        *bases,
        *feeds,
        spread,
        spread_other,
        weights,
        coeffs,
        plain,
        middle,
        middle_other,
        own_slab,
        needs=(group,),
    )
    vmem = pl.BlockSpec(memory_space=pltpu.VMEM)
    solved, states = pl.pallas_call(
        functools.partial(finish_body, bands, step),
        in_specs=[vmem] * (2 * bands + 5),
        out_specs=[pl.BlockSpec(memory_space=pltpu.HBM), vmem],
        out_shape=[
            jax.ShapeDtypeStruct((bands, nb, width), BF16),
            jax.ShapeDtypeStruct((bands, rank, width), F32),
        ],
        scratch_shapes=[
            pltpu.VMEM((bands, nb, width), BF16),
            pltpu.SemaphoreType.DMA((bands * len(blocks_of(nb)),)),
        ],
        compiler_params=pltpu.CompilerParams(vmem_limit_bytes=16 * 2**20),
        cost_estimate=pl.CostEstimate(flops=10**9, bytes_accessed=10**6, transcendentals=0),
        name="finish",
    )(*feeds, *gains, partial, offsets, near, arrived, carry_in)
    return (pivot_solution, turned(schur), solved, states)


def solution(mesh):
    return jax.shard_map(
        shards,
        mesh=mesh,
        in_specs=(
            P("col", "row", None, None),
            P("col", "row", None, None),
            P("col", None, None),
            P("col", None, None),
            P(),
            P("row", None, None),
            P("row", None, None),
            P(),
            P("row", None, None),
            P("row", None, None),
            P("row", None, None),
            P(None, "col"),
            P("row", None, "col"),
            P(None, "col"),
        ),
        out_specs=(
            P(None, "col"),
            P("row", "col", None),
            P("row", None, "col"),
            P("row", None, "col"),
        ),
        check_vma=False,
    )
```

```python
import functools

import jax
import jax.numpy as jnp
from jax import lax
from jax.experimental import pallas as pl
from jax.experimental.pallas import tpu as pltpu
from jax.sharding import PartitionSpec as P

F32 = jnp.float32
BF16 = jnp.bfloat16
LANES = 128
BLOCK = 256
NN = ((1,), (0,))
NT = ((1,), (1,))
TN = ((0,), (0,))


def halves(x):
    high = x.astype(BF16)
    return high, (x - high.astype(F32)).astype(BF16)


def bdot(a, b, dims=NN):
    return lax.dot_general(a, b, (dims, ((), ())), preferred_element_type=F32)


def dot2(a, b, dims=NN):
    high, low = halves(b)
    return bdot(a, high, dims) + bdot(a, low, dims)


def dot3(a, b, dims=NN):
    ah, al = halves(a)
    bh, bl = halves(b)
    return bdot(ah, bh, dims) + (bdot(ah, bl, dims) + bdot(al, bh, dims))


def vmem_call(body, outs, scratch=(), flops=10**7, name=None, limit=16):
    def call(*operands, needs=()):
        count = len(operands)

        def kernel(*refs):
            body(*refs[:count], *refs[count + len(needs) :])

        vmem = pl.BlockSpec(memory_space=pltpu.VMEM)
        return pl.pallas_call(
            kernel,
            in_specs=[vmem] * count + [pl.BlockSpec(memory_space=pl.ANY)] * len(needs),
            out_specs=[vmem] * len(outs),
            out_shape=[jax.ShapeDtypeStruct(s, d) for s, d in outs],
            scratch_shapes=list(scratch),
            compiler_params=pltpu.CompilerParams(vmem_limit_bytes=limit * 2**20),
            cost_estimate=pl.CostEstimate(flops=flops, bytes_accessed=10**6, transcendentals=0),
            name=name,
        )(*operands, *needs)

    return call


def held(x, *needs, weight=0):
    anywhere = pl.BlockSpec(memory_space=pl.ANY)
    return pl.pallas_call(
        lambda *refs: None,
        in_specs=[anywhere] * (1 + len(needs)),
        out_specs=anywhere,
        out_shape=jax.ShapeDtypeStruct(x.shape, x.dtype),
        input_output_aliases={0: 0},
        compiler_params=pltpu.CompilerParams(vmem_limit_bytes=2**20),
        cost_estimate=pl.CostEstimate(flops=weight, bytes_accessed=0, transcendentals=0),
        name="held",
    )(x, *needs)


def blocks_of(extent):
    size = min(BLOCK, extent)
    return [(start, start + size) for start in range(0, extent, size)]


def widen_body(row_left, out):
    half = out.shape[2]
    start = pl.multiple_of(lax.rem(lax.axis_index("row"), 2) * half, half)
    out[0] = row_left[:, pl.ds(start, half)].astype(F32)


def couple_body(
    tl_hbm, tr_hbm, rl_hbm, rr_hbm, sk_hbm, ready, own_hbm, msg_hbm, tl, tr, rl, rr, sk, own, msg, sems
):
    parity = lax.rem(lax.axis_index("col"), 2)
    rank, nb = rl.shape
    copies = [
        pltpu.make_async_copy(source, target, sems.at[index])
        for index, (source, target) in enumerate(
            (
                (tr_hbm, tr),
                (rr_hbm, rr),
                (tl_hbm, tl),
                (rl_hbm, rl),
                (sk_hbm, sk),
                (msg, msg_hbm),
                (own, own_hbm),
            )
        )
    ]
    for copy in copies[:5]:
        copy.start()
    for copy in copies[:5]:
        copy.wait()

    def crossed(band):
        coupling = bdot(tr[band], rr[...], NT)
        high, low = halves(coupling)
        both = bdot(jnp.concatenate([high, low], 1), tl[band], TN)
        return both[:rank] + both[rank:]

    msg[:, :nb] = crossed(1 - parity)
    probe = bdot(rl[...], sk[...], NT)
    msg[:, nb:] = jnp.concatenate([probe, jnp.zeros_like(probe)], 1)
    copies[5].start()
    own[...] = crossed(parity)
    copies[6].start()
    for copy in copies[5:]:
        copy.wait()


def sketch_body(pieces, x_own, sent, got, x_pair, *rest):
    outs, part = rest[:-1], rest[-1]
    col = lax.axis_index("col")
    parity = lax.rem(col, 2)
    place = col // 2
    rank, nb = x_own.shape
    own, other = x_own[...], got[:, :nb]
    probes = jnp.concatenate([sent[:, nb : nb + rank], got[:, nb : nb + rank]], 0)
    part[...] = dot3(probes, jnp.concatenate([own, other], 0), TN)
    x_pair[pl.ds(pl.multiple_of(parity * rank, rank), rank), :] = own
    x_pair[pl.ds(pl.multiple_of((1 - parity) * rank, rank), rank), :] = other
    slab = nb // pieces
    for step in range(pieces):
        start = pl.multiple_of(jnp.bitwise_xor(place, step) * slab, slab) if pieces > 1 else 0
        outs[step][...] = part[:, pl.ds(start, slab)]


def sum_body(*refs):
    total = refs[0][...]
    for part in refs[1:-1]:
        total = total + part[...]
    refs[-1][...] = total


def project_body(pieces, x_pair, *rest):
    slabs, (sk, crossed, gram) = rest[:pieces], rest[pieces:]
    place = lax.axis_index("col") // 2
    slab = slabs[0].shape[1]
    for step in range(pieces):
        start = pl.multiple_of(jnp.bitwise_xor(place, step) * slab, slab) if pieces > 1 else 0
        sk[:, pl.ds(start, slab)] = slabs[step][...]
    whole = sk[...]
    crossed[...] = dot3(whole, x_pair[...], NT)
    gram[...] = lax.dot_general(
        whole, whole, (NT, ((), ())), precision=lax.Precision.HIGHEST, preferred_element_type=F32
    )


def join_body(first, second, out):
    count = first.shape[0]
    out[:count] = first[...]
    out[count:] = second[...]


def narrow_body(order, *refs):
    blocks, out = refs[:-1], refs[-1]
    half = blocks[0].shape[-1]
    parity = lax.rem(lax.axis_index("col"), 2)
    near_start = pl.multiple_of(lax.rem(lax.axis_index("row"), 2) * half, half)
    far_start = pl.multiple_of(half - near_start, half)
    count = len(blocks) // 4
    for quarter, (side, start) in enumerate(
        ((parity, near_start), (1 - parity, near_start), (parity, far_start), (1 - parity, far_start))
    ):
        index = 0
        for chunk in blocks[quarter * count : (quarter + 1) * count]:
            for row in range(chunk.shape[0]):
                out[order[index], side, :, pl.ds(start, half)] = chunk[row].astype(BF16)
                index += 1


def factor_body(bands, gram, sketched, *refs):
    right_rows, (inverse_out, upper_out, slope_out) = refs[:bands], refs[bands:]
    parity = lax.rem(lax.axis_index("col"), 2)
    chosen = right_rows[0][...]
    for band in range(1, bands):
        chosen = jnp.where(parity == band, right_rows[band][...], chosen)
    slope_out[...] = dot3(chosen, sketched[...], NT)
    rank = gram.shape[0]
    lanes = 2 * rank
    group = 4
    tile = 8
    rows = lax.broadcasted_iota(jnp.int32, (rank, lanes), 0)
    cols = lax.broadcasted_iota(jnp.int32, (rank, lanes), 1)
    eye = jnp.where(cols == rows + rank, 1.0, 0.0).astype(F32)
    work = jnp.concatenate([gram[...], jnp.zeros((rank, rank), F32)], 1) + eye
    done = []
    scales = []
    for start in range(0, rank, group):
        top = (start // tile) * tile
        if start == top and start:
            done.append(work[:tile])
            work = work[tile:]
        ids = rows[top:]
        height = rank - top
        columns = [
            jnp.broadcast_to(work[:, start + j : start + j + 1], (height, lanes)) for j in range(group)
        ]
        for j in range(group):
            k = start + j
            at = k - top
            pivot = columns[j][at : at + 1, :]
            inverse = 1.0 / pivot
            scales.append(lax.rsqrt(pivot))
            factor = jnp.where(ids > k, columns[j] * inverse, 0.0)
            for later in range(j + 1, group):
                columns[later] = columns[later] - factor * columns[later][at : at + 1, :]
            work = work - factor * work[at : at + 1, :]
    done.append(work)
    whole = jnp.concatenate(done, 0) * jnp.concatenate(scales, 0)
    upper_out[...] = jnp.where(cols >= rows, whole, 0.0)[:, :rank]
    low = whole[:, rank:]
    inverse_out[...] = dot3(low, low, TN)


def scaled_body(groups, inverse, upper, slope, *rest):
    blocks, out = rest[:groups], rest[groups]
    two = jnp.concatenate(halves(inverse[...]), 0)
    rank, width = blocks[0].shape
    for step in range(groups):
        high, low = halves(blocks[step][...])
        both = bdot(two, high)
        out[:, step * width : (step + 1) * width] = both[:rank] + (both[rank:] + bdot(two[:rank], low))
    out[:, groups * width :] = jnp.concatenate([upper[...], slope[...]], 1)


def band_body(band, inverse, rhs, left, right, base, feed, offset, gain, right_rows):
    rank, nb = right.shape[1:]
    for first, last in blocks_of(nb):
        rows = inverse[band, first:last, :last]
        base[first:last, :] = bdot(rows, rhs[band, :last, :])
        both = bdot(rows, left[band, :, :last], NT)
        for side in range(2):
            high, low = halves(both[:, side * rank : (side + 1) * rank])
            feed[side, first:last, :] = jnp.concatenate([high, high, low], 1)
        right_rows[:, first:last] = bdot(right[band, :, first:], inverse[band, first:, first:last])
    two = jnp.concatenate(halves(right_rows[...]), 0)
    both = bdot(two, rhs[band])
    offset[...] = both[:rank] + both[rank:]
    both = bdot(two, left[band], NT)
    gain[...] = both[:rank] + both[rank:]


def spread_body(inverse, own, spread):
    parity = lax.rem(lax.axis_index("col"), 2)
    rank, nb = own.shape
    two = jnp.concatenate(halves(own[...]), 0)
    for first, last in blocks_of(nb):
        both = bdot(inverse[parity, first:last, :last], two[:, :last], NT)
        spread[:, first:last] = (both[:, :rank] + both[:, rank:]).T


def affine_body(bands, *refs):
    offset, gain = refs[:bands], refs[bands : 2 * bands]
    panel_right, pulled, carry, coeffs, plain, constant, matrix_out, high_out, low_out = refs[2 * bands :]
    rank = carry.shape[0]
    stacked = jnp.concatenate([panel_right[band] for band in range(bands)], 0)
    high, low = halves(pulled[...])
    high_out[...] = high
    low_out[...] = low
    both = bdot(stacked, high) + bdot(stacked, low)
    for band in range(bands):
        coeffs[band] = both[band * rank : (band + 1) * rank]
    constant_now = None
    matrix = None
    for band in range(bands):
        now = offset[band][...] - dot3(gain[band][:, :rank], coeffs[band])
        plain[band] = now
        feed = gain[band][:, rank:]
        constant_now = now - dot3(feed, constant_now) if band else now
        matrix = -dot3(feed, matrix) if band else -feed
    first = lax.axis_index("row") == 0
    constant[...] = constant_now + jnp.where(first, dot3(matrix, carry[...]), 0.0)
    matrix_out[...] = jnp.where(first, 0.0, matrix)


def stack3(x):
    high, low = halves(x)
    return jnp.concatenate([high, low, high], 0)


def weight_body(bands, *refs):
    gain = refs[:bands]
    own, other, wide, pulled_high, pulled_low, constant, matrix, weights, pack = refs[bands:]
    parity = lax.rem(lax.axis_index("col"), 2)
    rank = own.shape[0]
    count = wide.shape[0]
    width = pulled_high.shape[1]
    sides = [middle[:, :count] for middle in (own, other)]
    highs, lows = zip(*[halves(side) for side in sides])
    both = bdot(jnp.concatenate(highs + lows, 0), wide[...])
    high, low = halves(both[: bands * rank] + both[bands * rank :])
    upper = bdot(jnp.concatenate([high, low], 0), pulled_high[...])
    lower = bdot(high, pulled_low[...])
    own_first = upper[: bands * rank] + (upper[bands * rank :] + lower)
    own_weight, other_weight = own_first[:rank], own_first[rank:]
    ordered = []
    slopes = []
    for band in range(bands):
        ordered.append(jnp.where(parity == band, own_weight, other_weight))
        weights[band] = ordered[band]
        if band:
            slopes = [-dot3(gain[band][:, rank:], slope) for slope in slopes]
        ends = [middle[:, count + rank : count + 2 * rank] for middle in (own, other)]
        slopes.append(jnp.where(parity == band, ends[0], ends[1]))
    pack[:, :width] = constant[...] + dot3(jnp.concatenate(slopes, 1), jnp.concatenate(ordered, 0))
    pack[:, width:] = jnp.concatenate([matrix[...], jnp.zeros((rank, LANES - rank), F32)], 1)


def compose_body(bit, first, width, near, group, other, near_out, group_out):
    rank = group.shape[0]
    upper = lax.rem(lax.axis_index("row") // bit, 2) == 1

    def chained(then, before):
        moved = dot3(then[:, width : width + rank], before)
        lanes = lax.broadcasted_iota(jnp.int32, moved.shape, 1)
        return moved + jnp.where(lanes < width, then, 0.0)

    own, far = group[...], other[...]
    group_out[...] = chained(jnp.where(upper, own, far), jnp.where(upper, far, own))
    if first:
        lanes = lax.broadcasted_iota(jnp.int32, own.shape, 1)
        rows = lax.broadcasted_iota(jnp.int32, own.shape, 0)
        identity = jnp.where(lanes == rows + width, 1.0, 0.0).astype(F32)
        near_out[...] = jnp.where(upper, far, identity)
    else:
        near_out[...] = jnp.where(upper, chained(near[...], far), near[...])


def partial_body(bands, *refs):
    base, feed = refs[:bands], refs[bands : 2 * bands]
    own, other, weights, coeffs, plain, middle_own, middle_other, slab, out, offsets, schur = refs[2 * bands :]
    parity = lax.rem(lax.axis_index("col"), 2)
    nb = out.shape[1]
    rank = schur.shape[1]
    count, extent = slab.shape
    for band in range(bands):
        weight = weights[band]
        weight_three = stack3(weight)
        coeffs_three = stack3(coeffs[band])
        high, low = halves(jnp.where(parity == band, own[...], other[...]))
        spread = jnp.concatenate([high, high, low], 0)
        for first, last in blocks_of(nb):
            out[band, first:last, :] = (
                base[band][first:last, :]
                + bdot(spread[:, first:last], weight_three, TN)
                - bdot(feed[band][0, first:last, :], coeffs_three)
            )
        slope = jnp.where(
            parity == band,
            middle_own[:, count + rank : count + 2 * rank],
            middle_other[:, count + rank : count + 2 * rank],
        )
        offsets[band] = plain[band] + dot3(slope, weight)
    width = schur.shape[2]
    if extent == width:
        columns = slab[...]
    else:
        start = pl.multiple_of(lax.axis_index("col") * width, width)
        columns = slab[:, pl.ds(start, width)]
    for side, middle in ((parity, middle_own), (1 - parity, middle_other)):
        basis_side = dot3(middle[:, count : count + rank], middle[:, :count])
        both = bdot(jnp.concatenate(halves(basis_side), 0), columns)
        schur[side] = both[:rank] + both[rank:]


def finish_body(bands, bit, *refs):
    feed, gain = refs[:bands], refs[bands : 2 * bands]
    partial, offsets, near, other, carry, solved_hbm, states, solved, sems = refs[2 * bands :]
    _, nb, width = partial.shape
    rank = carry.shape[0]
    upper = lax.rem(lax.axis_index("row") // bit, 2) == 1
    prior = jnp.where(upper, other[...], carry[...])
    prior = dot3(near[:, width : width + rank], prior) + near[:, :width]
    copies = []
    for band in range(bands):
        three = stack3(prior)
        for first, last in blocks_of(nb):
            solved[band, first:last, :] = (
                partial[band, first:last, :] - bdot(feed[band][1, first:last, :], three)
            ).astype(BF16)
            copy = pltpu.make_async_copy(
                solved.at[band, first:last, :],
                solved_hbm.at[band, first:last, :],
                sems.at[len(copies)],
            )
            copy.start()
            copies.append(copy)
        prior = offsets[band] - dot3(gain[band][:, rank:], prior)
        states[band] = prior
    for copy in copies:
        copy.wait()


def shards(
    tile_left,
    tile_right,
    row_left,
    row_right,
    sketch,
    panel_left,
    panel_right,
    pivot_inverse,
    band_inverse,
    link_left,
    link_right,
    pivot_rhs,
    band_rhs,
    carry_in,
):
    cols = lax.axis_size("col")
    rows = lax.axis_size("row")
    groups = cols // 2
    col = lax.axis_index("col")
    bands, nb, rank = tile_left.shape[1:]
    width = pivot_rhs.shape[1]
    slab = nb // groups
    count = cols * rank

    def swap(x, step):
        return lax.ppermute(x, "col", [(c, c ^ step) for c in range(cols)])

    def row_swap(x, step):
        return lax.ppermute(x, "row", [(r, r ^ step) for r in range(rows)])

    def turned(x):
        return jnp.swapaxes(x, -1, -2)

    def joined(first, second, *needs):
        shape = (2 * first.shape[0],) + first.shape[1:]
        return vmem_call(join_body, [(shape, F32)], name="join")(first, second, needs=needs)[0]

    row_left_t = turned(row_left[0])
    (wide,) = vmem_call(widen_body, [((1, rank, nb // 2), F32)], name="widen")(row_left_t)
    order = [0]
    reach = groups // 2
    def hbm(count):
        return [pl.BlockSpec(memory_space=pltpu.HBM)] * count

    x_own, x_sent = pl.pallas_call(
        couple_body,
        in_specs=hbm(5) + [pl.BlockSpec(memory_space=pl.ANY)],
        out_specs=hbm(2),
        out_shape=[
            jax.ShapeDtypeStruct((rank, nb), F32),
            jax.ShapeDtypeStruct((rank, nb + LANES), F32),
        ],
        scratch_shapes=[pltpu.VMEM((bands, rank, nb), BF16)] * 2
        + [pltpu.VMEM((rank, nb), BF16)] * 3
        + [
            pltpu.VMEM((rank, nb), F32),
            pltpu.VMEM((rank, nb + LANES), F32),
            pltpu.SemaphoreType.DMA((7,)),
        ],
        compiler_params=pltpu.CompilerParams(vmem_limit_bytes=60 * 2**20),
        name="couple",
    )(
        turned(tile_left[0]),
        turned(tile_right[0]),
        row_left_t,
        turned(row_right[0]),
        turned(sketch),
        wide,
    )
    x_got = swap(x_sent, 1)

    pivot_solution = jnp.dot(pivot_inverse, pivot_rhs, preferred_element_type=F32).astype(BF16)
    pulled = bdot(pivot_inverse, pivot_solution, TN)

    def one_band(band, *needs):
        shapes = [(nb, width), (2, nb, 3 * rank), (rank, width), (rank, 2 * rank), (rank, nb)]
        return vmem_call(
            functools.partial(band_body, band),
            [(shape, BF16 if index == 1 else F32) for index, shape in enumerate(shapes)],
            flops=2 * 10**9,
            name="band",
        )(band_inverse, band_rhs, left_t, right_t, needs=needs)

    if reach:
        wide = joined(wide, swap(wide, 2 * reach))
        order = order + [place ^ reach for place in order]
        reach //= 2
    pieces = groups if slab % LANES == 0 else 1
    parts = vmem_call(
        functools.partial(sketch_body, pieces),
        [((2 * rank, nb), F32)] + [((rank, nb // pieces), F32)] * pieces,
        [pltpu.VMEM((rank, nb), F32)],
        name="sketch",
    )(x_own, x_sent, x_got, needs=(pulled, wide))
    x_pair, parts = parts[0], parts[1:]

    left_t = jnp.concatenate([turned(panel_left), turned(link_left)], 1)
    right_t = turned(link_right)
    whole_bands = []
    for band in range(bands):
        whole_bands.append(one_band(band, x_pair, *(last[-1] for last in whole_bands[-1:])))
    bases, feeds, offsets_in, gains, right_rows = zip(*whole_bands)
    coeffs, plain, constant, matrix, pulled_high, pulled_low = vmem_call(
        functools.partial(affine_body, bands),
        [((bands, rank, width), F32)] * 2
        + [((rank, width), F32), ((rank, rank), F32)]
        + [((nb, width), BF16)] * 2,
        name="affine",
    )(*offsets_in, *gains, turned(panel_right), pulled, carry_in)

    if pieces > 1:
        (total,) = vmem_call(sum_body, [((rank, slab), F32)], name="sum")(
            parts[0],
            *[swap(parts[step], 2 * step) for step in reversed(range(1, pieces))],
            needs=(wide, matrix),
        )
        slabs = [total] + [swap(total, 2 * step) for step in reversed(range(1, pieces))][::-1]
    else:
        members = [list(range(side, cols, 2)) for side in range(2)]
        total = lax.psum(parts[0], "col", axis_index_groups=members)
        slabs = [total]
    while reach:
        wide = joined(wide, swap(wide, 2 * reach), total)
        order = order + [place ^ reach for place in order]
        reach //= 2
    wide_other = held(swap(wide, 1), weight=0)
    sketched, crossed, gram = vmem_call(
        functools.partial(project_body, pieces),
        [((rank, nb), F32), ((rank, 2 * rank), F32), ((rank, rank), F32)],
        name="project",
    )(x_pair, *slabs)
    crossed_all = [crossed] + [swap(crossed, 2 * step) for step in reversed(range(1, groups))][::-1]
    inverse_gram, upper, slope = vmem_call(
        functools.partial(factor_body, bands), [((rank, rank), F32)] * 3, flops=3 * 10**10, name="factor"
    )(gram, sketched, *right_rows)
    (middle,) = vmem_call(
        functools.partial(scaled_body, groups), [((rank, count + LANES), F32)], name="scaled"
    )(inverse_gram, upper, slope, *crossed_all)
    middle_other = held(swap(middle, 1), weight=3 * 10**10)
    (spread,) = vmem_call(spread_body, [((rank, nb), F32)], name="spread")(
        band_inverse, sketched, needs=(middle, wide_other)
    )
    spread_other = swap(spread, 1)

    (wide,) = vmem_call(
        functools.partial(narrow_body, order), [((groups, 2, rank, nb), BF16)], name="narrow"
    )(wide, wide_other, row_swap(wide, 1), row_swap(wide_other, 1))
    wide = wide.reshape(count, nb)
    weights, pack = vmem_call(
        functools.partial(weight_body, bands),
        [((bands, rank, width), F32), ((rank, width + LANES), F32)],
        name="weight",
    )(*gains, middle, middle_other, wide, pulled_high, pulled_low, constant, matrix)

    near, group = pack, pack
    step = 1
    while 2 * step < rows:
        near, group = vmem_call(
            functools.partial(compose_body, step, step == 1, width),
            [((rank, width + LANES), F32)] * 2,
            name="compose",
        )(near, group, row_swap(group, step))
        step *= 2
    arrived = row_swap(group[:, :width], step)

    own_slab = wide
    if (nb // cols) % LANES:
        own_slab = lax.dynamic_slice_in_dim(wide, col * (nb // cols), nb // cols, 1)
    partial, offsets, schur = vmem_call(
        functools.partial(partial_body, bands),
        [
            ((bands, nb, width), F32),
            ((bands, rank, width), F32),
            ((bands, rank, nb // cols), F32),
        ],
        flops=10**9,
        name="partial",
    )(
        *bases,
        *feeds,
        spread,
        spread_other,
        weights,
        coeffs,
        plain,
        middle,
        middle_other,
        own_slab,
        needs=(group,),
    )
    vmem = pl.BlockSpec(memory_space=pltpu.VMEM)
    solved, states = pl.pallas_call(
        functools.partial(finish_body, bands, step),
        in_specs=[vmem] * (2 * bands + 5),
        out_specs=[pl.BlockSpec(memory_space=pltpu.HBM), vmem],
        out_shape=[
            jax.ShapeDtypeStruct((bands, nb, width), BF16),
            jax.ShapeDtypeStruct((bands, rank, width), F32),
        ],
        scratch_shapes=[
            pltpu.VMEM((bands, nb, width), BF16),
            pltpu.SemaphoreType.DMA((bands * len(blocks_of(nb)),)),
        ],
        compiler_params=pltpu.CompilerParams(vmem_limit_bytes=16 * 2**20),
        cost_estimate=pl.CostEstimate(flops=10**9, bytes_accessed=10**6, transcendentals=0),
        name="finish",
    )(*feeds, *gains, partial, offsets, near, arrived, carry_in)
    return (pivot_solution, turned(schur), solved, states)


def solution(mesh):
    return jax.shard_map(
        shards,
        mesh=mesh,
        in_specs=(
            P("col", "row", None, None),
            P("col", "row", None, None),
            P("col", None, None),
            P("col", None, None),
            P(),
            P("row", None, None),
            P("row", None, None),
            P(),
            P("row", None, None),
            P("row", None, None),
            P("row", None, None),
            P(None, "col"),
            P("row", None, "col"),
            P(None, "col"),
        ),
        out_specs=(
            P(None, "col"),
            P("row", "col", None),
            P("row", None, "col"),
            P("row", None, "col"),
        ),
        check_vma=False,
    )
```
